32 devices in a mesh: grp: 1, col: 32 (over z, y, x, core).
Axes of the slice: x: 2, y: 2, z: 4, core: 2. Of those that a mesh axis runs over, the one named last changes fastest.
Arguments:
- pair: bfloat16 [16, 1024, 128], P('grp', 'col'), may hold values from -6 to 6
- w_query: bfloat16 [128, 128], replicated, may hold values from -0.5 to 0.5
- w_kv: bfloat16 [128, 256], replicated, may hold values from -0.5 to 0.5
- w_gate: bfloat16 [128, 128], replicated, may hold values from -0.5 to 0.5
- w_out: bfloat16 [128, 128], replicated, may hold values from -0.5 to 0.5
- pair_bias: bfloat16 [4, 1024, 1024], P('grp', 'col'), may hold values from -8 to 300
- lengths: int32 [1], P('grp'), may hold values from 512 to 1024
Outputs:
- update: bfloat16 [16, 1024, 128], P('grp', 'col')
The draws below stay inside these ranges and needn't reach their ends.
All inputs are finite; a program needn't handle non-finite values.
Results may differ from the reference program's by a relative error of at most 0.0081.
Values may be sent and summed in bfloat16 or wider, within the bound.
A program may use at most 128 MiB of HBM per device.

```python
import jax
import jax.numpy as jnp
from jax import lax

CHANNELS = 128
HEADS = 4
ROWS = 16
N_TOK = 1024


def draw_pair_bias(key, part):
    base = jnp.clip(2.0 * jax.random.normal(key, (HEADS, N_TOK, N_TOK), jnp.float32), -8.0, 8.0)
    return base.astype(jnp.bfloat16)


def block_scale(stream_key, dims, cuts, smallest, top_value):
    def one(axis_at, blocks):
        heights = jax.random.uniform(jax.random.fold_in(jax.random.fold_in(stream_key, 6), axis_at), (blocks,), jnp.float32, smallest / len(cuts), top_value / len(cuts))
        return jnp.repeat(jnp.exp(heights), dims[axis_at] // blocks).reshape((-1,) + (1,) * (len(dims) - axis_at - 1))

    loudness = one(*cuts[0])
    for cut in cuts[1:]:
        loudness = loudness * one(*cut)
    return loudness


def normal_values(key, dims, deviation, reach, split=(), kind=jnp.bfloat16):
    result = deviation * jax.random.normal(key, dims, jnp.float32)
    if split:
        result = result * block_scale(key, dims, split, -0.22, 0.18)
    return jnp.clip(result, -reach, reach).astype(kind)


def setup_inputs(seed: int = 0, part: int = 0) -> dict:
    key_of = jax.random.split(jax.random.key(seed), 8)
    part_splits = jax.random.split(jax.random.fold_in(key_of[7], part), 8)
    pair = normal_values(part_splits[0], (ROWS, N_TOK, CHANNELS), 1.0, 6.0, ((1, 32),))
    w_query = normal_values(key_of[1], (CHANNELS, CHANNELS), CHANNELS ** -0.5, 0.5)
    w_kv = normal_values(key_of[2], (CHANNELS, 2 * CHANNELS), CHANNELS ** -0.5, 0.5)
    w_gate = normal_values(key_of[3], (CHANNELS, CHANNELS), CHANNELS ** -0.5, 0.5)
    w_out = normal_values(key_of[4], (CHANNELS, CHANNELS), CHANNELS ** -0.5, 0.5)
    pair_bias = draw_pair_bias(jax.random.fold_in(jax.random.fold_in(key_of[7], part), 71), part)
    lengths = jax.random.randint(part_splits[6], (1,), N_TOK // 2, N_TOK + 1).astype(jnp.int32)
    return {"pair": pair, "w_query": w_query, "w_kv": w_kv, "w_gate": w_gate, "w_out": w_out, "pair_bias": pair_bias, "lengths": lengths}


def normalize(pair_row):
    values_f = pair_row.astype(jnp.float32)
    mean_val = lax.optimization_barrier(jnp.mean(values_f, axis=-1, keepdims=True))
    centred = values_f - mean_val
    variance = lax.optimization_barrier(jnp.mean(centred * centred, axis=-1, keepdims=True))
    return (centred * lax.rsqrt(variance + 1e-05)).astype(jnp.bfloat16)

def reference(pair, w_query, w_kv, w_gate, w_out, pair_bias, lengths):
    chan_count = pair.shape[-1]
    head_width = chan_count // HEADS
    bias_query = jnp.swapaxes(pair_bias, 1, 2).astype(jnp.float32)
    key_mask = jnp.where(jnp.arange(N_TOK) < lengths[0], 0.0, -1000000000.0).astype(jnp.float32)

    def one_row(pair_row):
        normed = normalize(pair_row)
        queries = (jnp.dot(normed, w_query, preferred_element_type=jnp.float32) * head_width ** (-0.5)).astype(jnp.bfloat16)
        queries = queries.reshape(N_TOK, HEADS, head_width)
        key_value = jnp.dot(normed, w_kv, preferred_element_type=jnp.float32).astype(jnp.bfloat16)
        key_tile = key_value[:, :chan_count].reshape(N_TOK, HEADS, head_width)
        value_tile = key_value[:, chan_count:].reshape(N_TOK, HEADS, head_width)
        gate_act = jax.nn.sigmoid(jnp.dot(normed, w_gate, preferred_element_type=jnp.float32))
        scores = jnp.einsum('jhd,khd->hjk', queries.astype(jnp.float32), key_tile.astype(jnp.float32))
        scores = scores + bias_query + key_mask
        row_max = lax.optimization_barrier(jnp.max(scores, axis=-1, keepdims=True))
        expon = jnp.exp(scores - row_max)
        total = lax.optimization_barrier(jnp.sum(expon, axis=-1))
        rounded = lax.optimization_barrier(expon.astype(jnp.bfloat16)).astype(jnp.float32)
        numer = jnp.einsum('hjk,khd->jhd', rounded, value_tile.astype(jnp.float32))
        attended = numer / jnp.transpose(total)[:, :, None]
        hidden = (gate_act * attended.reshape(N_TOK, chan_count)).astype(jnp.bfloat16)
        return jnp.dot(hidden, w_out, preferred_element_type=jnp.float32).astype(jnp.bfloat16)
    return lax.map(one_row, pair)
```

```python
import functools

import jax
import jax.numpy as jnp
from jax import lax
from jax.experimental import pallas as pl
from jax.experimental.pallas import tpu as pltpu
from jax.sharding import PartitionSpec as P

HEADS = 4
MESH = pl.DeviceIdType.MESH
F32 = jnp.float32
BF16 = jnp.bfloat16
LOG2E = 1.4426950408889634
NT = (((1,), (1,)), ((), ()))
TN = (((0,), (0,)), ((), ()))


def dot(lhs, rhs):
    return jnp.dot(lhs, rhs, preferred_element_type=F32)


def dot_nt(lhs, rhs):
    return lax.dot_general(lhs, rhs, NT, preferred_element_type=F32)


def transposed(weight):
    return weight.astype(F32).T.astype(BF16)


def body(
    line, pair_ref, wq_ref, wkv_ref, wg_ref, wo_ref, bias_ref, len_ref, out_ref,
    gath, swap, bsend, bgath, bias_f, amat, gate, acc, run_max, run_sum, upd,
    wvt_ref, recv, zsend, nsend, fsend, bs_sem, br_sem, core_s, core_r,
):
    rows, cols, chan = pair_ref.shape
    half_rows, cols2 = rows // 2, 2 * cols
    quarter = half_rows // 2
    width = chan // HEADS
    lanes = HEADS * cols2
    chips = 4 * line

    me = lax.axis_index("col")
    core = lax.rem(me, 2)
    chip = me // 2
    z = chip // 4
    xy = lax.rem(chip, 4)
    sibling = me + 1 - 2 * core
    x_line = xy + 1 - 2 * lax.rem(xy, 2)
    y_line = lax.rem(xy + 2, 4)
    diag = 3 - xy
    near = (x_line, y_line)
    far = (y_line, x_line)

    def device(z_at, xy_at):
        return {"col": (z_at * 4 + xy_at) * 2 + core}

    barrier = pltpu.get_barrier_semaphore()

    def greet(k, carry):
        other = lax.rem(chip + k, chips)
        pl.semaphore_signal(barrier, inc=1, device_id={"col": other * 2 + core}, device_id_type=MESH)
        return carry

    lax.fori_loop(1, chips, greet, 0)
    pl.semaphore_signal(barrier, inc=1, device_id={"col": sibling}, device_id_type=MESH)

    def normalized(first):
        values = pair_ref[pl.ds(first, half_rows)].astype(F32)
        centred = values - jnp.mean(values, axis=-1, keepdims=True)
        variance = jnp.mean(centred * centred, axis=-1, keepdims=True)
        return (centred * lax.rsqrt(variance + 1e-05)).astype(BF16)

    own_cols = pl.ds(pl.multiple_of(core * cols, cols), cols)
    swap[...] = normalized((1 - core) * half_rows)
    gath[xy, z, :, own_cols, :] = normalized(core * half_rows)

    pl.semaphore_wait(barrier, chips)

    swap_copy = pltpu.make_async_remote_copy(
        src_ref=swap, dst_ref=gath.at[xy, z, :, own_cols, :],
        send_sem=core_s.at[0], recv_sem=core_r.at[0],
        device_id={"col": sibling}, device_id_type=MESH,
    )
    swap_copy.start()

    low = lax.broadcasted_iota(jnp.int32, (cols, 2 * cols2), 1) < cols2
    for pair_at in range(chips // 2):
        parts = [
            bias_ref[h, :, pair_at * 2 * cols2 : (pair_at + 1) * 2 * cols2].astype(F32)
            for h in range(HEADS)
        ]
        rolled = [pltpu.roll(part, cols2, 1) for part in parts]
        for h in range(0, HEADS, 2):
            span = slice(h * cols2, (h + 2) * cols2)
            bsend[2 * pair_at, :, span] = jnp.where(low, parts[h], rolled[h + 1]).astype(BF16)
            bsend[2 * pair_at + 1, :, span] = jnp.where(low, rolled[h], parts[h + 1]).astype(BF16)

    swap_copy.wait_recv()

    def block_copy(half, xy_at, z_at, target, send_sem):
        block = gath.at[xy_at, z_at, pl.ds(half * quarter, quarter)]
        return pltpu.make_async_remote_copy(
            src_ref=block, dst_ref=block, send_sem=send_sem, recv_sem=recv.at[half, xy_at, z_at],
            device_id=target, device_id_type=MESH,
        )

    def up(half, z_at):
        return block_copy(half, xy, z_at, device(z + 1, xy), zsend.at[half, 0, z_at])

    def down(half, z_at):
        return block_copy(half, xy, z_at, device(z - 1, xy), zsend.at[half, 1, z_at])

    def to_near(half, z_at):
        return block_copy(half, xy, z_at, device(z, near[half]), nsend.at[half, z_at])

    def to_far(half, which, z_at):
        from_line = (xy, near[half])[which]
        return block_copy(half, from_line, z_at, device(z, far[half]), fsend.at[half, which, z_at])

    def arrived(half, xy_at, z_at):
        block_copy(half, xy_at, z_at, device(z, near[half]), nsend.at[half, z_at]).wait_recv()

    for half in range(2):
        pl.when(z + 1 < line)(lambda half=half: up(half, z).start())
        pl.when(z > 0)(lambda half=half: down(half, z).start())
        to_near(half, z).start()
        to_far(half, 0, z).start()

    def bias_copy(other, slot):
        return pltpu.make_async_remote_copy(
            src_ref=bsend.at[other], dst_ref=bgath.at[lax.rem(slot, 4), slot // 4, own_cols, :],
            send_sem=bs_sem.at[other], recv_sem=br_sem.at[slot],
            device_id={"col": other * 2 + core}, device_id_type=MESH,
        )

    def send_bias(k, carry):
        bias_copy(lax.rem(chip + k, chips), chip).start()
        return carry

    lax.fori_loop(1, chips, send_bias, 0)
    bgath[xy, z, own_cols, :] = bsend[chip]

    wqt = transposed(wq_ref[...])
    wgt = transposed(wg_ref[...])
    wvt_ref[...] = transposed(wkv_ref[:, chan:])
    w_key = wkv_ref[:, :chan]
    same_head = (
        lax.broadcasted_iota(jnp.int32, (chan, lanes), 0) // width
        == lax.broadcasted_iota(jnp.int32, (chan, lanes), 1) // cols2
    )

    def prepare(r, carry):
        own = gath[xy, z, r]
        repeated = jnp.concatenate([own] * HEADS, axis=0)
        queries = (dot_nt(wqt, repeated) * width ** (-0.5)).astype(BF16).astype(F32)
        queries = jnp.where(same_head, queries, 0.0).astype(BF16)
        amat[r] = (dot(w_key, queries) * LOG2E).astype(BF16)
        gate[r] = jax.nn.sigmoid(dot_nt(wgt, own))
        return carry

    lax.fori_loop(0, half_rows, prepare, 0)

    def pass_far(half, z_at):
        arrived(half, near[half], z_at)
        to_far(half, 1, z_at).start()

    def pass_line(s):
        def lower():
            for half in range(2):
                arrived(half, xy, z - s)
                pl.when(z + 1 < line)(lambda: up(half, z - s).start())
                to_near(half, z - s).start()
                to_far(half, 0, z - s).start()

        def upper():
            for half in range(2):
                arrived(half, xy, z + s)
                pl.when(z > 0)(lambda: down(half, z + s).start())
                to_near(half, z + s).start()
                to_far(half, 0, z + s).start()

        pl.when(z >= s)(lower)
        pl.when(z + s < line)(upper)

    def pass_near(s):
        def lower():
            for half in range(2):
                pass_far(half, z - s)

        def upper():
            for half in range(2):
                pass_far(half, z + s)

        pl.when(z >= s)(lower)
        if s:
            pl.when(z + s < line)(upper)

    for s in range(1, line):
        pass_line(s)
        pass_near(s - 1)
    pass_near(line - 1)

    def wait_bias(k, carry):
        other = lax.rem(chip + k, chips)
        bias_copy(other, other).wait_recv()
        return carry

    lax.fori_loop(1, chips, wait_bias, 0)
    bias_swap = pltpu.make_async_remote_copy(
        src_ref=bgath.at[:, :, own_cols, :], dst_ref=bgath.at[:, :, own_cols, :],
        send_sem=core_s.at[1], recv_sem=core_r.at[1],
        device_id={"col": sibling}, device_id_type=MESH,
    )
    bias_swap.start()
    bias_swap.wait_recv()

    limit = len_ref[0]

    def spread_bias(k, carry):
        line_at, z_at = k // line, lax.rem(k, line)
        first = (z_at * 4 + line_at) * cols2
        position = first + lax.broadcasted_iota(jnp.int32, (cols2, lanes), 0)
        mask = jnp.where(position < limit, 0.0, -1000000000.0)
        bias_f[line_at, z_at] = (bgath[line_at, z_at].astype(F32) + mask) * LOG2E
        return carry

    lax.fori_loop(0, chips, spread_bias, 0)

    run_max[...] = jnp.full_like(run_max, -1e30)
    run_sum[...] = jnp.zeros_like(run_sum)
    acc[...] = jnp.zeros_like(acc)
    group = 4 if line % 4 == 0 else 1
    keys = group * cols2

    def fold(half, lines):
        wvt = wvt_ref[...]

        def one(step, carry):
            r = half * quarter + step // (line // group)
            z_at = pl.ds(lax.rem(step, line // group) * group, group)
            tiles = [gath[at, z_at, r].reshape(keys, chan) for at in lines]
            scores = [
                dot(tile, amat[r]) + bias_f[at, z_at].reshape(keys, lanes)
                for tile, at in zip(tiles, lines)
            ]
            old_max = run_max[r]
            new_max = old_max
            for part in scores:
                new_max = jnp.maximum(new_max, jnp.max(part, axis=0, keepdims=True))
            rescale = jnp.exp2(old_max - new_max)
            total = run_sum[r] * rescale
            result = acc[r] * rescale
            for part, tile in zip(scores, tiles):
                expon = jnp.exp2(part - new_max)
                total = total + jnp.sum(expon, axis=0, keepdims=True)
                result = result + dot(dot_nt(wvt, tile).astype(BF16), expon.astype(BF16))
            run_max[r] = new_max
            run_sum[r] = total
            acc[r] = result
            return carry

        steps = quarter * (line // group)
        lax.fori_loop(0, steps, one, 0, unroll=2)

    def wait_line(half, at):
        for z_at in range(line):
            arrived(half, at, z_at)

    for half in range(2):
        fold(half, (xy, near[half]))
    for half in range(2):
        wait_line(half, far[half])
        fold(half, (far[half],))

    other_cols = pl.ds(pl.multiple_of((1 - core) * cols, cols), cols)

    def out_copy(half):
        return pltpu.make_async_remote_copy(
            src_ref=upd.at[pl.ds(half * quarter, quarter), other_cols, :],
            dst_ref=out_ref.at[pl.ds(core * half_rows + half * quarter, quarter)],
            send_sem=core_s.at[2 + half], recv_sem=core_r.at[2 + half],
            device_id={"col": sibling}, device_id_type=MESH,
        )

    for half in range(2):
        wait_line(half, diag)
        fold(half, (diag,))

        def finish(step, carry):
            r = half * quarter + step
            result = acc[r] / run_sum[r]
            parts = []
            for h in range(HEADS):
                block = result[h * width : (h + 1) * width, (h // 2) * 2 * cols2 : (h // 2 + 1) * 2 * cols2]
                if h % 2:
                    block = pltpu.roll(block, cols2, 1)
                parts.append(block[:, :cols2])
            attended = jnp.concatenate(parts, axis=0)
            hidden = (gate[r] * attended).T.astype(BF16)
            upd[r] = dot(hidden, wo_ref[...]).astype(BF16)
            return carry

        lax.fori_loop(0, quarter, finish, 0, unroll=2)
        out_copy(half).start()
        out_ref[pl.ds(core * half_rows + half * quarter, quarter)] = upd[
            pl.ds(half * quarter, quarter), own_cols, :
        ]

    for half in range(2):
        out_copy(half).wait()
        for z_at in range(line):
            pl.when((z + 1 < line) & (z >= z_at))(lambda: up(half, z_at).wait_send())
            pl.when((z > 0) & (z <= z_at))(lambda: down(half, z_at).wait_send())
            to_near(half, z_at).wait_send()
            to_far(half, 0, z_at).wait_send()
            to_far(half, 1, z_at).wait_send()
    swap_copy.wait_send()
    bias_swap.wait_send()

    def drain_bias(k, carry):
        bias_copy(lax.rem(chip + k, chips), chip).wait_send()
        return carry

    lax.fori_loop(1, chips, drain_bias, 0)


def solution(mesh):
    chips = mesh.shape["col"] // 2
    line = chips // 4

    def on_device(pair, w_query, w_kv, w_gate, w_out, pair_bias, lengths):
        rows, cols, chan = pair.shape
        half_rows, cols2 = rows // 2, 2 * cols
        quarter = half_rows // 2
        lanes = HEADS * cols2
        vmem = pl.BlockSpec(memory_space=pltpu.VMEM)
        dma = pltpu.SemaphoreType.DMA
        return pl.pallas_call(
            functools.partial(body, line),
            out_shape=jax.ShapeDtypeStruct(pair.shape, BF16),
            in_specs=[vmem] * 6 + [pl.BlockSpec(memory_space=pltpu.SMEM)],
            out_specs=vmem,
            scratch_shapes=[
                pltpu.VMEM((4, line, half_rows, cols2, chan), BF16),
                pltpu.VMEM((half_rows, cols, chan), BF16),
                pltpu.VMEM((chips, cols, lanes), BF16),
                pltpu.VMEM((4, line, cols2, lanes), BF16),
                pltpu.VMEM((4, line, cols2, lanes), F32),
                pltpu.VMEM((half_rows, chan, lanes), BF16),
                pltpu.VMEM((half_rows, chan, cols2), F32),
                pltpu.VMEM((half_rows, chan, lanes), F32),
                pltpu.VMEM((half_rows, 1, lanes), F32),
                pltpu.VMEM((half_rows, 1, lanes), F32),
                pltpu.VMEM((half_rows, cols2, chan), BF16),
                pltpu.VMEM((chan, chan), BF16),
                dma((2, 4, line)),
                dma((2, 2, line)),
                dma((2, line)),
                dma((2, 2, line)),
                dma((chips,)),
                dma((chips,)),
                dma((4,)),
                dma((4,)),
            ],
            compiler_params=pltpu.CompilerParams(
                collective_id=0, has_side_effects=True, vmem_limit_bytes=48 * 1024 * 1024
            ),
            cost_estimate=pl.CostEstimate(flops=3 * 10**9, bytes_accessed=10**6, transcendentals=2 * 10**6),
        )(pair, w_query, w_kv, w_gate, w_out, pair_bias, lengths)

    in_specs = (P("grp", "col", None), P(), P(), P(), P(), P("grp", "col", None), P("grp"))
    return jax.shard_map(
        on_device, mesh=mesh, in_specs=in_specs, out_specs=P("grp", "col", None), check_vma=False
    )
```

```python
import functools

import jax
import jax.numpy as jnp
from jax import lax
from jax.experimental import pallas as pl
from jax.experimental.pallas import tpu as pltpu
from jax.sharding import PartitionSpec as P

HEADS = 4
MESH = pl.DeviceIdType.MESH
F32 = jnp.float32
BF16 = jnp.bfloat16
LOG2E = 1.4426950408889634
NT = (((1,), (1,)), ((), ()))
TN = (((0,), (0,)), ((), ()))


def dot(lhs, rhs):
    return jnp.dot(lhs, rhs, preferred_element_type=F32)


def dot_nt(lhs, rhs):
    return lax.dot_general(lhs, rhs, NT, preferred_element_type=F32)


def transposed(weight):
    return weight.astype(F32).T.astype(BF16)


def body(
    line, pair_in, wq_in, wkv_in, wg_in, wo_in, bias_in, len_ref, out_ref,
    pair_ref, bias_ref, wq_ref, wkv_ref, wg_ref, wo_ref, load_sem,
    gath, swap, bsend, bgath, bias_f, amat, gate, acc, run_max, run_sum, upd,
    wvt_ref, recv, zsend, nsend, fsend, bs_sem, br_sem, core_s, core_r,
):
    rows, cols, chan = pair_ref.shape
    half_rows, cols2 = rows // 2, 2 * cols
    quarter = half_rows // 2
    width = chan // HEADS
    lanes = HEADS * cols2
    chips = 4 * line

    me = lax.axis_index("col")
    core = lax.rem(me, 2)
    chip = me // 2
    z = chip // 4
    xy = lax.rem(chip, 4)
    sibling = me + 1 - 2 * core
    x_line = xy + 1 - 2 * lax.rem(xy, 2)
    y_line = lax.rem(xy + 2, 4)
    diag = 3 - xy
    near = (x_line, y_line)
    far = (y_line, x_line)

    def device(z_at, xy_at):
        return {"col": (z_at * 4 + xy_at) * 2 + core}

    loads = [
        pltpu.make_async_copy(source, target, load_sem.at[at])
        for at, (source, target) in enumerate((
            (pair_in, pair_ref), (bias_in, bias_ref), (wq_in, wq_ref),
            (wkv_in, wkv_ref), (wg_in, wg_ref), (wo_in, wo_ref),
        ))
    ]
    for load in loads:
        load.start()

    barrier = pltpu.get_barrier_semaphore()

    def greet(k, carry):
        other = lax.rem(chip + k, chips)
        pl.semaphore_signal(barrier, inc=1, device_id={"col": other * 2 + core}, device_id_type=MESH)
        return carry

    lax.fori_loop(1, chips, greet, 0)
    pl.semaphore_signal(barrier, inc=1, device_id={"col": sibling}, device_id_type=MESH)

    def normalized(first):
        values = pair_ref[pl.ds(first, half_rows)].astype(F32)
        centred = values - jnp.mean(values, axis=-1, keepdims=True)
        variance = jnp.mean(centred * centred, axis=-1, keepdims=True)
        return (centred * lax.rsqrt(variance + 1e-05)).astype(BF16)

    loads[0].wait()
    own_cols = pl.ds(pl.multiple_of(core * cols, cols), cols)
    swap[...] = normalized((1 - core) * half_rows)
    gath[xy, z, :, own_cols, :] = normalized(core * half_rows)

    pl.semaphore_wait(barrier, chips)

    swap_copy = pltpu.make_async_remote_copy(
        src_ref=swap, dst_ref=gath.at[xy, z, :, own_cols, :],
        send_sem=core_s.at[0], recv_sem=core_r.at[0],
        device_id={"col": sibling}, device_id_type=MESH,
    )
    swap_copy.start()

    loads[1].wait()
    low = lax.broadcasted_iota(jnp.int32, (cols, 2 * cols2), 1) < cols2
    for pair_at in range(chips // 2):
        parts = [
            bias_ref[h, :, pair_at * 2 * cols2 : (pair_at + 1) * 2 * cols2].astype(F32)
            for h in range(HEADS)
        ]
        rolled = [pltpu.roll(part, cols2, 1) for part in parts]
        for h in range(0, HEADS, 2):
            span = slice(h * cols2, (h + 2) * cols2)
            bsend[2 * pair_at, :, span] = jnp.where(low, parts[h], rolled[h + 1]).astype(BF16)
            bsend[2 * pair_at + 1, :, span] = jnp.where(low, rolled[h], parts[h + 1]).astype(BF16)

    swap_copy.wait_recv()

    def block_copy(half, xy_at, z_at, target, send_sem):
        block = gath.at[xy_at, z_at, pl.ds(half * quarter, quarter)]
        return pltpu.make_async_remote_copy(
            src_ref=block, dst_ref=block, send_sem=send_sem, recv_sem=recv.at[half, xy_at, z_at],
            device_id=target, device_id_type=MESH,
        )

    def up(half, z_at):
        return block_copy(half, xy, z_at, device(z + 1, xy), zsend.at[half, 0, z_at])

    def down(half, z_at):
        return block_copy(half, xy, z_at, device(z - 1, xy), zsend.at[half, 1, z_at])

    def to_near(half, z_at):
        return block_copy(half, xy, z_at, device(z, near[half]), nsend.at[half, z_at])

    def to_far(half, which, z_at):
        from_line = (xy, near[half])[which]
        return block_copy(half, from_line, z_at, device(z, far[half]), fsend.at[half, which, z_at])

    def arrived(half, xy_at, z_at):
        block_copy(half, xy_at, z_at, device(z, near[half]), nsend.at[half, z_at]).wait_recv()

    for half in range(2):
        pl.when(z + 1 < line)(lambda half=half: up(half, z).start())
        pl.when(z > 0)(lambda half=half: down(half, z).start())
        to_near(half, z).start()
        to_far(half, 0, z).start()

    def bias_copy(other, slot):
        return pltpu.make_async_remote_copy(
            src_ref=bsend.at[other], dst_ref=bgath.at[lax.rem(slot, 4), slot // 4, own_cols, :],
            send_sem=bs_sem.at[other], recv_sem=br_sem.at[slot],
            device_id={"col": other * 2 + core}, device_id_type=MESH,
        )

    def send_bias(k, carry):
        bias_copy(lax.rem(chip + k, chips), chip).start()
        return carry

    lax.fori_loop(1, chips, send_bias, 0)
    bgath[xy, z, own_cols, :] = bsend[chip]

    for load in loads[2:]:
        load.wait()
    wqt = transposed(wq_ref[...])
    wgt = transposed(wg_ref[...])
    wvt_ref[...] = transposed(wkv_ref[:, chan:])
    w_key = wkv_ref[:, :chan]
    same_head = (
        lax.broadcasted_iota(jnp.int32, (chan, lanes), 0) // width
        == lax.broadcasted_iota(jnp.int32, (chan, lanes), 1) // cols2
    )

    def prepare(r, carry):
        own = gath[xy, z, r]
        repeated = jnp.concatenate([own] * HEADS, axis=0)
        queries = (dot_nt(wqt, repeated) * width ** (-0.5)).astype(BF16).astype(F32)
        queries = jnp.where(same_head, queries, 0.0).astype(BF16)
        amat[r] = (dot(w_key, queries) * LOG2E).astype(BF16)
        gate[r] = jax.nn.sigmoid(dot_nt(wgt, own))
        return carry

    lax.fori_loop(0, half_rows, prepare, 0)

    def pass_far(half, z_at):
        arrived(half, near[half], z_at)
        to_far(half, 1, z_at).start()

    def pass_line(s):
        def lower():
            for half in range(2):
                arrived(half, xy, z - s)
                pl.when(z + 1 < line)(lambda: up(half, z - s).start())
                to_near(half, z - s).start()
                to_far(half, 0, z - s).start()

        def upper():
            for half in range(2):
                arrived(half, xy, z + s)
                pl.when(z > 0)(lambda: down(half, z + s).start())
                to_near(half, z + s).start()
                to_far(half, 0, z + s).start()

        pl.when(z >= s)(lower)
        pl.when(z + s < line)(upper)

    def pass_near(s):
        def lower():
            for half in range(2):
                pass_far(half, z - s)

        def upper():
            for half in range(2):
                pass_far(half, z + s)

        pl.when(z >= s)(lower)
        if s:
            pl.when(z + s < line)(upper)

    for s in range(1, line):
        pass_line(s)
        pass_near(s - 1)
    pass_near(line - 1)

    def wait_bias(k, carry):
        other = lax.rem(chip + k, chips)
        bias_copy(other, other).wait_recv()
        return carry

    lax.fori_loop(1, chips, wait_bias, 0)
    bias_swap = pltpu.make_async_remote_copy(
        src_ref=bgath.at[:, :, own_cols, :], dst_ref=bgath.at[:, :, own_cols, :],
        send_sem=core_s.at[1], recv_sem=core_r.at[1],
        device_id={"col": sibling}, device_id_type=MESH,
    )
    bias_swap.start()
    bias_swap.wait_recv()

    limit = len_ref[0]

    def spread_bias(k, carry):
        line_at, z_at = k // line, lax.rem(k, line)
        first = (z_at * 4 + line_at) * cols2
        position = first + lax.broadcasted_iota(jnp.int32, (cols2, lanes), 0)
        mask = jnp.where(position < limit, 0.0, -1000000000.0)
        bias_f[line_at, z_at] = (bgath[line_at, z_at].astype(F32) + mask) * LOG2E
        return carry

    lax.fori_loop(0, chips, spread_bias, 0)

    run_max[...] = jnp.full_like(run_max, -1e30)
    run_sum[...] = jnp.zeros_like(run_sum)
    acc[...] = jnp.zeros_like(acc)
    group = 4 if line % 4 == 0 else 1
    keys = group * cols2

    def fold(half, lines):
        wvt = wvt_ref[...]

        def one(step, carry):
            r = half * quarter + step // (line // group)
            z_at = pl.ds(lax.rem(step, line // group) * group, group)
            tiles = [gath[at, z_at, r].reshape(keys, chan) for at in lines]
            scores = [
                dot(tile, amat[r]) + bias_f[at, z_at].reshape(keys, lanes)
                for tile, at in zip(tiles, lines)
            ]
            old_max = run_max[r]
            new_max = old_max
            for part in scores:
                new_max = jnp.maximum(new_max, jnp.max(part, axis=0, keepdims=True))
            rescale = jnp.exp2(old_max - new_max)
            total = run_sum[r] * rescale
            result = acc[r] * rescale
            for part, tile in zip(scores, tiles):
                expon = jnp.exp2(part - new_max)
                total = total + jnp.sum(expon, axis=0, keepdims=True)
                result = result + dot(dot_nt(wvt, tile).astype(BF16), expon.astype(BF16))
            run_max[r] = new_max
            run_sum[r] = total
            acc[r] = result
            return carry

        steps = quarter * (line // group)
        lax.fori_loop(0, steps, one, 0, unroll=2)

    def wait_line(half, at):
        for z_at in range(line):
            arrived(half, at, z_at)

    for half in range(2):
        fold(half, (xy, near[half]))
    for half in range(2):
        wait_line(half, far[half])
        fold(half, (far[half],))

    other_cols = pl.ds(pl.multiple_of((1 - core) * cols, cols), cols)

    def out_copy(half):
        return pltpu.make_async_remote_copy(
            src_ref=upd.at[pl.ds(half * quarter, quarter), other_cols, :],
            dst_ref=out_ref.at[pl.ds(core * half_rows + half * quarter, quarter)],
            send_sem=core_s.at[2 + half], recv_sem=core_r.at[2 + half],
            device_id={"col": sibling}, device_id_type=MESH,
        )

    for half in range(2):
        wait_line(half, diag)
        fold(half, (diag,))

        def finish(step, carry):
            r = half * quarter + step
            result = acc[r] / run_sum[r]
            parts = []
            for h in range(HEADS):
                block = result[h * width : (h + 1) * width, (h // 2) * 2 * cols2 : (h // 2 + 1) * 2 * cols2]
                if h % 2:
                    block = pltpu.roll(block, cols2, 1)
                parts.append(block[:, :cols2])
            attended = jnp.concatenate(parts, axis=0)
            hidden = (gate[r] * attended).T.astype(BF16)
            upd[r] = dot(hidden, wo_ref[...]).astype(BF16)
            return carry

        lax.fori_loop(0, quarter, finish, 0, unroll=2)
        out_copy(half).start()
        out_ref[pl.ds(core * half_rows + half * quarter, quarter)] = upd[
            pl.ds(half * quarter, quarter), own_cols, :
        ]

    for half in range(2):
        out_copy(half).wait()
        for z_at in range(line):
            pl.when((z + 1 < line) & (z >= z_at))(lambda: up(half, z_at).wait_send())
            pl.when((z > 0) & (z <= z_at))(lambda: down(half, z_at).wait_send())
            to_near(half, z_at).wait_send()
            to_far(half, 0, z_at).wait_send()
            to_far(half, 1, z_at).wait_send()
    swap_copy.wait_send()
    bias_swap.wait_send()

    def drain_bias(k, carry):
        bias_copy(lax.rem(chip + k, chips), chip).wait_send()
        return carry

    lax.fori_loop(1, chips, drain_bias, 0)


def solution(mesh):
    chips = mesh.shape["col"] // 2
    line = chips // 4

    def on_device(pair, w_query, w_kv, w_gate, w_out, pair_bias, lengths):
        rows, cols, chan = pair.shape
        half_rows, cols2 = rows // 2, 2 * cols
        quarter = half_rows // 2
        lanes = HEADS * cols2
        vmem = pl.BlockSpec(memory_space=pltpu.VMEM)
        dma = pltpu.SemaphoreType.DMA
        return pl.pallas_call(
            functools.partial(body, line),
            out_shape=jax.ShapeDtypeStruct(pair.shape, BF16),
            in_specs=[pl.BlockSpec(memory_space=pltpu.HBM)] * 6 + [pl.BlockSpec(memory_space=pltpu.SMEM)],
            out_specs=vmem,
            scratch_shapes=[
                pltpu.VMEM(pair.shape, BF16),
                pltpu.VMEM(pair_bias.shape, BF16),
                pltpu.VMEM(w_query.shape, BF16),
                pltpu.VMEM(w_kv.shape, BF16),
                pltpu.VMEM(w_gate.shape, BF16),
                pltpu.VMEM(w_out.shape, BF16),
                dma((6,)),
                pltpu.VMEM((4, line, half_rows, cols2, chan), BF16),
                pltpu.VMEM((half_rows, cols, chan), BF16),
                pltpu.VMEM((chips, cols, lanes), BF16),
                pltpu.VMEM((4, line, cols2, lanes), BF16),
                pltpu.VMEM((4, line, cols2, lanes), F32),
                pltpu.VMEM((half_rows, chan, lanes), BF16),
                pltpu.VMEM((half_rows, chan, cols2), F32),
                pltpu.VMEM((half_rows, chan, lanes), F32),
                pltpu.VMEM((half_rows, 1, lanes), F32),
                pltpu.VMEM((half_rows, 1, lanes), F32),
                pltpu.VMEM((half_rows, cols2, chan), BF16),
                pltpu.VMEM((chan, chan), BF16),
                dma((2, 4, line)),
                dma((2, 2, line)),
                dma((2, line)),
                dma((2, 2, line)),
                dma((chips,)),
                dma((chips,)),
                dma((4,)),
                dma((4,)),
            ],
            compiler_params=pltpu.CompilerParams(
                collective_id=0, has_side_effects=True, vmem_limit_bytes=48 * 1024 * 1024
            ),
            cost_estimate=pl.CostEstimate(flops=3 * 10**9, bytes_accessed=10**6, transcendentals=2 * 10**6),
        )(pair, w_query, w_kv, w_gate, w_out, pair_bias, lengths)

    in_specs = (P("grp", "col", None), P(), P(), P(), P(), P("grp", "col", None), P("grp"))
    return jax.shard_map(
        on_device, mesh=mesh, in_specs=in_specs, out_specs=P("grp", "col", None), check_vma=False
    )
```

```python
import functools

import jax
import jax.numpy as jnp
from jax import lax
from jax.experimental import pallas as pl
from jax.experimental.pallas import tpu as pltpu
from jax.sharding import PartitionSpec as P

HEADS = 4
MESH = pl.DeviceIdType.MESH
F32 = jnp.float32
BF16 = jnp.bfloat16
LOG2E = 1.4426950408889634
NT = (((1,), (1,)), ((), ()))
TN = (((0,), (0,)), ((), ()))


def dot(lhs, rhs):
    return jnp.dot(lhs, rhs, preferred_element_type=F32)


def dot_nt(lhs, rhs):
    return lax.dot_general(lhs, rhs, NT, preferred_element_type=F32)


def transposed(weight):
    return weight.astype(F32).T.astype(BF16)


def body(
    line, pair_in, wq_in, wkv_in, wg_in, wo_in, bias_in, len_ref, out_ref,
    pair_ref, bias_ref, wq_ref, wkv_ref, wg_ref, wo_ref, load_sem,
    gath, swap, bsend, bgath, bias_f, queries, gate, acc, run_max, run_sum, upd,
    wvt_ref, recv, zsend, nsend, fsend, bs_sem, br_sem, core_s, core_r,
):
    rows, cols, chan = pair_ref.shape
    half_rows, cols2 = rows // 2, 2 * cols
    quarter = half_rows // 2
    width = chan // HEADS
    lanes = HEADS * cols2
    chips = 4 * line

    me = lax.axis_index("col")
    core = lax.rem(me, 2)
    chip = me // 2
    z = chip // 4
    xy = lax.rem(chip, 4)
    sibling = me + 1 - 2 * core
    x_line = xy + 1 - 2 * lax.rem(xy, 2)
    y_line = lax.rem(xy + 2, 4)
    diag = 3 - xy
    near = (x_line, y_line)
    far = (y_line, x_line)

    def device(z_at, xy_at):
        return {"col": (z_at * 4 + xy_at) * 2 + core}

    loads = [
        pltpu.make_async_copy(source, target, load_sem.at[at])
        for at, (source, target) in enumerate((
            (pair_in, pair_ref), (bias_in, bias_ref), (wq_in, wq_ref),
            (wkv_in, wkv_ref), (wg_in, wg_ref), (wo_in, wo_ref),
        ))
    ]
    for load in loads:
        load.start()

    barrier = pltpu.get_barrier_semaphore()

    def greet(k, carry):
        other = lax.rem(chip + k, chips)
        pl.semaphore_signal(barrier, inc=1, device_id={"col": other * 2 + core}, device_id_type=MESH)
        return carry

    lax.fori_loop(1, chips, greet, 0)
    pl.semaphore_signal(barrier, inc=1, device_id={"col": sibling}, device_id_type=MESH)

    def normalized(first):
        values = pair_ref[pl.ds(first, half_rows)].astype(F32)
        centred = values - jnp.mean(values, axis=-1, keepdims=True)
        variance = jnp.mean(centred * centred, axis=-1, keepdims=True)
        return (centred * lax.rsqrt(variance + 1e-05)).astype(BF16)

    loads[0].wait()
    own_cols = pl.ds(pl.multiple_of(core * cols, cols), cols)
    swap[...] = normalized((1 - core) * half_rows)
    gath[xy, z, :, own_cols, :] = normalized(core * half_rows)

    pl.semaphore_wait(barrier, chips)

    swap_copy = pltpu.make_async_remote_copy(
        src_ref=swap, dst_ref=gath.at[xy, z, :, own_cols, :],
        send_sem=core_s.at[0], recv_sem=core_r.at[0],
        device_id={"col": sibling}, device_id_type=MESH,
    )
    swap_copy.start()

    loads[1].wait()
    low = lax.broadcasted_iota(jnp.int32, (cols, 2 * cols2), 1) < cols2
    for pair_at in range(chips // 2):
        parts = [
            bias_ref[h, :, pair_at * 2 * cols2 : (pair_at + 1) * 2 * cols2].astype(F32)
            for h in range(HEADS)
        ]
        rolled = [pltpu.roll(part, cols2, 1) for part in parts]
        for h in range(0, HEADS, 2):
            span = slice(h * cols2, (h + 2) * cols2)
            bsend[2 * pair_at, :, span] = jnp.where(low, parts[h], rolled[h + 1]).astype(BF16)
            bsend[2 * pair_at + 1, :, span] = jnp.where(low, rolled[h], parts[h + 1]).astype(BF16)

    swap_copy.wait_recv()

    def block_copy(half, xy_at, z_at, target, send_sem):
        block = gath.at[xy_at, z_at, pl.ds(half * quarter, quarter)]
        return pltpu.make_async_remote_copy(
            src_ref=block, dst_ref=block, send_sem=send_sem, recv_sem=recv.at[half, xy_at, z_at],
            device_id=target, device_id_type=MESH,
        )

    def up(half, z_at):
        return block_copy(half, xy, z_at, device(z + 1, xy), zsend.at[half, 0, z_at])

    def down(half, z_at):
        return block_copy(half, xy, z_at, device(z - 1, xy), zsend.at[half, 1, z_at])

    def to_near(half, z_at):
        return block_copy(half, xy, z_at, device(z, near[half]), nsend.at[half, z_at])

    def to_far(half, which, z_at):
        from_line = (xy, near[half])[which]
        return block_copy(half, from_line, z_at, device(z, far[half]), fsend.at[half, which, z_at])

    def arrived(half, xy_at, z_at):
        block_copy(half, xy_at, z_at, device(z, near[half]), nsend.at[half, z_at]).wait_recv()

    for half in range(2):
        pl.when(z + 1 < line)(lambda half=half: up(half, z).start())
        pl.when(z > 0)(lambda half=half: down(half, z).start())
        to_near(half, z).start()
        to_far(half, 0, z).start()

    def bias_copy(other, slot):
        return pltpu.make_async_remote_copy(
            src_ref=bsend.at[other], dst_ref=bgath.at[lax.rem(slot, 4), slot // 4, own_cols, :],
            send_sem=bs_sem.at[other], recv_sem=br_sem.at[slot],
            device_id={"col": other * 2 + core}, device_id_type=MESH,
        )

    def send_bias(k, carry):
        bias_copy(lax.rem(chip + k, chips), chip).start()
        return carry

    lax.fori_loop(1, chips, send_bias, 0)
    bgath[xy, z, own_cols, :] = bsend[chip]

    for load in loads[2:]:
        load.wait()
    wqt = transposed(wq_ref[...])
    wgt = transposed(wg_ref[...])
    wvt_ref[...] = transposed(wkv_ref[:, chan:])
    same_head = (
        lax.broadcasted_iota(jnp.int32, (chan, lanes), 0) // width
        == lax.broadcasted_iota(jnp.int32, (chan, lanes), 1) // cols2
    )

    def prepare(r, carry):
        own = gath[xy, z, r]
        repeated = jnp.concatenate([own] * HEADS, axis=0)
        own_query = (dot_nt(wqt, repeated) * width ** (-0.5)).astype(BF16).astype(F32)
        own_query = jnp.where(same_head, own_query, 0.0).astype(BF16)
        queries[r] = own_query
        gate[r] = jax.nn.sigmoid(dot_nt(wgt, own))
        return carry

    lax.fori_loop(0, half_rows, prepare, 0)

    def pass_far(half, z_at):
        arrived(half, near[half], z_at)
        to_far(half, 1, z_at).start()

    def pass_line(s):
        def lower():
            for half in range(2):
                arrived(half, xy, z - s)
                pl.when(z + 1 < line)(lambda: up(half, z - s).start())
                to_near(half, z - s).start()
                to_far(half, 0, z - s).start()

        def upper():
            for half in range(2):
                arrived(half, xy, z + s)
                pl.when(z > 0)(lambda: down(half, z + s).start())
                to_near(half, z + s).start()
                to_far(half, 0, z + s).start()

        pl.when(z >= s)(lower)
        pl.when(z + s < line)(upper)

    def pass_near(s):
        def lower():
            for half in range(2):
                pass_far(half, z - s)

        def upper():
            for half in range(2):
                pass_far(half, z + s)

        pl.when(z >= s)(lower)
        if s:
            pl.when(z + s < line)(upper)

    for s in range(1, line):
        pass_line(s)
        pass_near(s - 1)
    pass_near(line - 1)

    def wait_bias(k, carry):
        other = lax.rem(chip + k, chips)
        bias_copy(other, other).wait_recv()
        return carry

    lax.fori_loop(1, chips, wait_bias, 0)
    bias_swap = pltpu.make_async_remote_copy(
        src_ref=bgath.at[:, :, own_cols, :], dst_ref=bgath.at[:, :, own_cols, :],
        send_sem=core_s.at[1], recv_sem=core_r.at[1],
        device_id={"col": sibling}, device_id_type=MESH,
    )
    bias_swap.start()
    bias_swap.wait_recv()

    limit = len_ref[0]

    def spread_bias(k, carry):
        line_at, z_at = k // line, lax.rem(k, line)
        first = (z_at * 4 + line_at) * cols2
        position = first + lax.broadcasted_iota(jnp.int32, (cols2, lanes), 0)
        mask = jnp.where(position < limit, 0.0, -1000000000.0)
        bias_f[line_at, z_at] = (bgath[line_at, z_at].astype(F32) + mask) * LOG2E
        return carry

    lax.fori_loop(0, chips, spread_bias, 0)

    run_max[...] = jnp.full_like(run_max, -1e30)
    run_sum[...] = jnp.zeros_like(run_sum)
    acc[...] = jnp.zeros_like(acc)
    group = 4 if line % 4 == 0 else 1
    keys = group * cols2
    row_step = 2

    def fold(half, lines):
        wvt = wvt_ref[...]
        w_key = wkv_ref[:, :chan]

        def one_group(rows_at, part_at):
            z_at = pl.ds(part_at * group, group)
            olds = [(run_max[r], run_sum[r], acc[r]) for r in rows_at]
            news = []
            for r, (old_max, old_sum, old_acc) in zip(rows_at, olds):
                tiles = [gath[at, z_at, r].reshape(keys, chan) for at in lines]
                scores = [
                    dot(dot(tile, w_key).astype(BF16), queries[r]) * LOG2E
                    + bias_f[at, z_at].reshape(keys, lanes)
                    for tile, at in zip(tiles, lines)
                ]
                new_max = old_max
                for part in scores:
                    new_max = jnp.maximum(new_max, jnp.max(part, axis=0, keepdims=True))
                rescale = jnp.exp2(old_max - new_max)
                total = old_sum * rescale
                result = old_acc * rescale
                for part, tile in zip(scores, tiles):
                    expon = jnp.exp2(part - new_max)
                    total = total + jnp.sum(expon, axis=0, keepdims=True)
                    result = result + dot(dot_nt(wvt, tile).astype(BF16), expon.astype(BF16))
                news.append((new_max, total, result))
            for r, new in zip(rows_at, news):
                run_max[r], run_sum[r], acc[r] = new

        for first in range(half * quarter, (half + 1) * quarter, row_step):
            rows_at = range(first, first + row_step)
            if line == group:
                one_group(rows_at, 0)
            else:
                lax.fori_loop(0, line // group, lambda at, _: one_group(rows_at, at), None)

    def wait_line(half, at):
        for z_at in range(line):
            arrived(half, at, z_at)

    for half in range(2):
        fold(half, (xy, near[half]))
    for half in range(2):
        wait_line(half, far[half])
        fold(half, (far[half],))

    other_cols = pl.ds(pl.multiple_of((1 - core) * cols, cols), cols)

    def out_copy(half):
        return pltpu.make_async_remote_copy(
            src_ref=upd.at[pl.ds(half * quarter, quarter), other_cols, :],
            dst_ref=out_ref.at[pl.ds(core * half_rows + half * quarter, quarter)],
            send_sem=core_s.at[2 + half], recv_sem=core_r.at[2 + half],
            device_id={"col": sibling}, device_id_type=MESH,
        )

    for half in range(2):
        wait_line(half, diag)
        fold(half, (diag,))

        hiddens = []
        for r in range(half * quarter, (half + 1) * quarter):
            result = acc[r] * (1.0 / run_sum[r])
            parts = []
            for h in range(HEADS):
                pair_of = slice((h // 2) * 2 * cols2, (h // 2 + 1) * 2 * cols2)
                block = result[h * width : (h + 1) * width, pair_of]
                if h % 2:
                    block = pltpu.roll(block, cols2, 1)
                parts.append(block[:, :cols2])
            attended = jnp.concatenate(parts, axis=0)
            hiddens.append((gate[r] * attended).T.astype(BF16))
        update = dot(jnp.concatenate(hiddens, axis=0), wo_ref[...]).astype(BF16)
        upd[pl.ds(half * quarter, quarter)] = update.reshape(quarter, cols2, chan)
        out_copy(half).start()
        out_ref[pl.ds(core * half_rows + half * quarter, quarter)] = upd[
            pl.ds(half * quarter, quarter), own_cols, :
        ]

    for half in range(2):
        out_copy(half).wait()
        for z_at in range(line):
            pl.when((z + 1 < line) & (z >= z_at))(lambda: up(half, z_at).wait_send())
            pl.when((z > 0) & (z <= z_at))(lambda: down(half, z_at).wait_send())
            to_near(half, z_at).wait_send()
            to_far(half, 0, z_at).wait_send()
            to_far(half, 1, z_at).wait_send()
    swap_copy.wait_send()
    bias_swap.wait_send()

    def drain_bias(k, carry):
        bias_copy(lax.rem(chip + k, chips), chip).wait_send()
        return carry

    lax.fori_loop(1, chips, drain_bias, 0)


def solution(mesh):
    chips = mesh.shape["col"] // 2
    line = chips // 4

    def on_device(pair, w_query, w_kv, w_gate, w_out, pair_bias, lengths):
        rows, cols, chan = pair.shape
        half_rows, cols2 = rows // 2, 2 * cols
        quarter = half_rows // 2
        lanes = HEADS * cols2
        vmem = pl.BlockSpec(memory_space=pltpu.VMEM)
        dma = pltpu.SemaphoreType.DMA
        return pl.pallas_call(
            functools.partial(body, line),
            out_shape=jax.ShapeDtypeStruct(pair.shape, BF16),
            in_specs=[pl.BlockSpec(memory_space=pl.ANY)] * 6 + [pl.BlockSpec(memory_space=pltpu.SMEM)],
            out_specs=vmem,
            scratch_shapes=[
                pltpu.VMEM(pair.shape, BF16),
                pltpu.VMEM(pair_bias.shape, BF16),
                pltpu.VMEM(w_query.shape, BF16),
                pltpu.VMEM(w_kv.shape, BF16),
                pltpu.VMEM(w_gate.shape, BF16),
                pltpu.VMEM(w_out.shape, BF16),
                dma((6,)),
                pltpu.VMEM((4, line, half_rows, cols2, chan), BF16),
                pltpu.VMEM((half_rows, cols, chan), BF16),
                pltpu.VMEM((chips, cols, lanes), BF16),
                pltpu.VMEM((4, line, cols2, lanes), BF16),
                pltpu.VMEM((4, line, cols2, lanes), F32),
                pltpu.VMEM((half_rows, chan, lanes), BF16),
                pltpu.VMEM((half_rows, chan, cols2), F32),
                pltpu.VMEM((half_rows, chan, lanes), F32),
                pltpu.VMEM((half_rows, 1, lanes), F32),
                pltpu.VMEM((half_rows, 1, lanes), F32),
                pltpu.VMEM((half_rows, cols2, chan), BF16),
                pltpu.VMEM((chan, chan), BF16),
                dma((2, 4, line)),
                dma((2, 2, line)),
                dma((2, line)),
                dma((2, 2, line)),
                dma((chips,)),
                dma((chips,)),
                dma((4,)),
                dma((4,)),
            ],
            compiler_params=pltpu.CompilerParams(
                collective_id=0, has_side_effects=True
            ),
            cost_estimate=pl.CostEstimate(flops=3 * 10**9, bytes_accessed=10**6, transcendentals=2 * 10**6),
        )(pair, w_query, w_kv, w_gate, w_out, pair_bias, lengths)

    in_specs = (P("grp", "col", None), P(), P(), P(), P(), P("grp", "col", None), P("grp"))
    return jax.shard_map(
        on_device, mesh=mesh, in_specs=in_specs, out_specs=P("grp", "col", None), check_vma=False
    )
```

```python
import functools

import jax
import jax.numpy as jnp
from jax import lax
from jax.experimental import pallas as pl
from jax.experimental.pallas import tpu as pltpu
from jax.sharding import PartitionSpec as P

HEADS = 4
MESH = pl.DeviceIdType.MESH
F32 = jnp.float32
BF16 = jnp.bfloat16
LOG2E = 1.4426950408889634
NT = (((1,), (1,)), ((), ()))
TN = (((0,), (0,)), ((), ()))


def dot(lhs, rhs):
    return jnp.dot(lhs, rhs, preferred_element_type=F32)


def dot_nt(lhs, rhs):
    return lax.dot_general(lhs, rhs, NT, preferred_element_type=F32)


def transposed(weight):
    return weight.astype(F32).T.astype(BF16)


def body(
    line, pair_in, wq_in, wkv_in, wg_in, wo_in, bias_in, len_ref, out_ref,
    pair_ref, bias_ref, wq_ref, wkv_ref, wg_ref, wo_ref, load_sem,
    gath, swap, bsend, bgath, bias_f, queries, gate, acc, run_max, run_sum, upd,
    wvt_ref, recv, zsend, nsend, fsend, bs_sem, br_sem, core_s, core_r,
):
    rows, cols, chan = pair_ref.shape
    half_rows, cols2 = rows // 2, 2 * cols
    quarter = half_rows // 2
    width = chan // HEADS
    lanes = HEADS * cols2
    chips = 4 * line

    me = lax.axis_index("col")
    core = lax.rem(me, 2)
    chip = me // 2
    z = chip // 4
    xy = lax.rem(chip, 4)
    sibling = me + 1 - 2 * core
    x_line = xy + 1 - 2 * lax.rem(xy, 2)
    y_line = lax.rem(xy + 2, 4)
    diag = 3 - xy
    near = (x_line, y_line)
    far = (y_line, x_line)

    def device(z_at, xy_at):
        return {"col": (z_at * 4 + xy_at) * 2 + core}

    loads = [
        pltpu.make_async_copy(source, target, load_sem.at[at])
        for at, (source, target) in enumerate((
            (pair_in, pair_ref), (bias_in, bias_ref), (wq_in, wq_ref),
            (wkv_in, wkv_ref), (wg_in, wg_ref), (wo_in, wo_ref),
        ))
    ]
    for load in loads:
        load.start()

    barrier = pltpu.get_barrier_semaphore()

    def greet(k, carry):
        other = lax.rem(chip + k, chips)
        pl.semaphore_signal(barrier, inc=1, device_id={"col": other * 2 + core}, device_id_type=MESH)
        return carry

    lax.fori_loop(1, chips, greet, 0)
    pl.semaphore_signal(barrier, inc=1, device_id={"col": sibling}, device_id_type=MESH)

    def normalized(first):
        values = pair_ref[pl.ds(first, half_rows)].astype(F32)
        centred = values - jnp.mean(values, axis=-1, keepdims=True)
        variance = jnp.mean(centred * centred, axis=-1, keepdims=True)
        return (centred * lax.rsqrt(variance + 1e-05)).astype(BF16)

    loads[0].wait()
    own_cols = pl.ds(pl.multiple_of(core * cols, cols), cols)
    swap[...] = normalized((1 - core) * half_rows)
    gath[xy, z, :, own_cols, :] = normalized(core * half_rows)

    pl.semaphore_wait(barrier, chips)

    swap_copy = pltpu.make_async_remote_copy(
        src_ref=swap, dst_ref=gath.at[xy, z, :, own_cols, :],
        send_sem=core_s.at[0], recv_sem=core_r.at[0],
        device_id={"col": sibling}, device_id_type=MESH,
    )
    swap_copy.start()

    loads[1].wait()
    low = lax.broadcasted_iota(jnp.int32, (cols, 2 * cols2), 1) < cols2
    for pair_at in range(chips // 2):
        parts = [
            bias_ref[h, :, pair_at * 2 * cols2 : (pair_at + 1) * 2 * cols2].astype(F32)
            for h in range(HEADS)
        ]
        rolled = [pltpu.roll(part, cols2, 1) for part in parts]
        for h in range(0, HEADS, 2):
            span = slice(h * cols2, (h + 2) * cols2)
            bsend[2 * pair_at, :, span] = jnp.where(low, parts[h], rolled[h + 1]).astype(BF16)
            bsend[2 * pair_at + 1, :, span] = jnp.where(low, rolled[h], parts[h + 1]).astype(BF16)

    swap_copy.wait_recv()

    def block_copy(half, xy_at, z_at, target, send_sem):
        block = gath.at[xy_at, z_at, pl.ds(half * quarter, quarter)]
        return pltpu.make_async_remote_copy(
            src_ref=block, dst_ref=block, send_sem=send_sem, recv_sem=recv.at[half, xy_at, z_at],
            device_id=target, device_id_type=MESH,
        )

    def up(half, z_at):
        return block_copy(half, xy, z_at, device(z + 1, xy), zsend.at[half, 0, z_at])

    def down(half, z_at):
        return block_copy(half, xy, z_at, device(z - 1, xy), zsend.at[half, 1, z_at])

    def to_near(half, z_at):
        return block_copy(half, xy, z_at, device(z, near[half]), nsend.at[half, z_at])

    def to_far(half, which, z_at):
        from_line = (xy, near[half])[which]
        return block_copy(half, from_line, z_at, device(z, far[half]), fsend.at[half, which, z_at])

    def arrived(half, xy_at, z_at):
        block_copy(half, xy_at, z_at, device(z, near[half]), nsend.at[half, z_at]).wait_recv()

    for half in range(2):
        pl.when(z + 1 < line)(lambda half=half: up(half, z).start())
        pl.when(z > 0)(lambda half=half: down(half, z).start())
        to_near(half, z).start()
        to_far(half, 0, z).start()

    def bias_copy(other, slot):
        return pltpu.make_async_remote_copy(
            src_ref=bsend.at[other], dst_ref=bgath.at[lax.rem(slot, 4), slot // 4, own_cols, :],
            send_sem=bs_sem.at[other], recv_sem=br_sem.at[slot],
            device_id={"col": other * 2 + core}, device_id_type=MESH,
        )

    def bias_peers(line_at, first, act):
        def one(k, carry):
            act(lax.rem(z + k, line) * 4 + line_at)
            return carry

        lax.fori_loop(first, line, one, 0)

    all_lines = ((xy, 1), (x_line, 0), (y_line, 0), (diag, 0))
    for line_at, first in all_lines:
        bias_peers(line_at, first, lambda other: bias_copy(other, chip).start())
    bgath[xy, z, own_cols, :] = bsend[chip]

    for load in loads[2:]:
        load.wait()
    wqt = transposed(wq_ref[...])
    wgt = transposed(wg_ref[...])
    wvt_ref[...] = transposed(wkv_ref[:, chan:])
    same_head = (
        lax.broadcasted_iota(jnp.int32, (chan, lanes), 0) // width
        == lax.broadcasted_iota(jnp.int32, (chan, lanes), 1) // cols2
    )

    def prepare(r, carry):
        own = gath[xy, z, r]
        repeated = jnp.concatenate([own] * HEADS, axis=0)
        own_query = (dot_nt(wqt, repeated) * width ** (-0.5)).astype(BF16).astype(F32)
        own_query = jnp.where(same_head, own_query, 0.0).astype(BF16)
        queries[r] = own_query
        gate[r] = jax.nn.sigmoid(dot_nt(wgt, own))
        return carry

    lax.fori_loop(0, half_rows, prepare, 0)

    def pass_far(half, z_at):
        arrived(half, near[half], z_at)
        to_far(half, 1, z_at).start()

    def pass_line(s):
        def lower():
            for half in range(2):
                arrived(half, xy, z - s)
                pl.when(z + 1 < line)(lambda: up(half, z - s).start())
                to_near(half, z - s).start()
                to_far(half, 0, z - s).start()

        def upper():
            for half in range(2):
                arrived(half, xy, z + s)
                pl.when(z > 0)(lambda: down(half, z + s).start())
                to_near(half, z + s).start()
                to_far(half, 0, z + s).start()

        pl.when(z >= s)(lower)
        pl.when(z + s < line)(upper)

    def pass_near(s):
        def lower():
            for half in range(2):
                pass_far(half, z - s)

        def upper():
            for half in range(2):
                pass_far(half, z + s)

        pl.when(z >= s)(lower)
        if s:
            pl.when(z + s < line)(upper)

    def bias_swap(at):
        line_at = all_lines[at][0]
        return pltpu.make_async_remote_copy(
            src_ref=bgath.at[line_at, :, own_cols, :], dst_ref=bgath.at[line_at, :, own_cols, :],
            send_sem=core_s.at[3 + at], recv_sem=core_r.at[3 + at],
            device_id={"col": sibling}, device_id_type=MESH,
        )

    def start_bias(at):
        line_at, first = all_lines[at]
        bias_peers(line_at, first, lambda other: bias_copy(other, other).wait_recv())
        bias_swap(at).start()

    limit = len_ref[0]

    def spread_bias(at):
        bias_swap(at).wait_recv()
        line_at = all_lines[at][0]

        def one(z_at, carry):
            first = (z_at * 4 + line_at) * cols2
            position = first + lax.broadcasted_iota(jnp.int32, (cols2, lanes), 0)
            mask = jnp.where(position < limit, 0.0, -1000000000.0)
            bias_f[line_at, z_at] = (bgath[line_at, z_at].astype(F32) + mask) * LOG2E
            return carry

        lax.fori_loop(0, line, one, 0)

    run_max[...] = jnp.full_like(run_max, -1e30)
    run_sum[...] = jnp.zeros_like(run_sum)
    acc[...] = jnp.zeros_like(acc)
    group = line // 2
    keys = group * cols2
    own_part = z // group
    per_pair = 2 * cols2

    def fold(half, line_at, part):
        first = half * quarter
        z_at = pl.ds(part * group, group)
        tiles = [gath[line_at, z_at, first + r].reshape(keys, chan) for r in range(quarter)]
        olds = [(run_max[first + r], run_sum[first + r], acc[first + r]) for r in range(quarter)]
        bias_tile = bias_f[line_at, z_at].reshape(keys, lanes)
        together = jnp.concatenate(tiles, axis=0)
        all_keys = dot(together, wkv_ref[:, :chan]).astype(BF16)
        all_values = dot_nt(wvt_ref[...], together).astype(BF16)
        news = []
        for r, (old_max, old_sum, old_acc) in enumerate(olds):
            span = slice(r * keys, (r + 1) * keys)
            scores = dot(all_keys[span], queries[first + r]) * LOG2E + bias_tile
            new_max = jnp.maximum(old_max, jnp.max(scores, axis=0, keepdims=True))
            rescale = jnp.exp2(old_max - new_max)
            expon = jnp.exp2(scores - new_max)
            total = old_sum * rescale + jnp.sum(expon, axis=0, keepdims=True)
            product = dot(all_values[:, span], expon.astype(BF16))
            result = []
            for h in range(HEADS):
                at = slice(h * width, (h + 1) * width)
                pair_of = slice((h // 2) * per_pair, (h // 2 + 1) * per_pair)
                result.append(old_acc[at] * rescale[:, pair_of] + product[at, pair_of])
            news.append((new_max, total, jnp.concatenate(result, axis=0)))
        for r, new in enumerate(news):
            run_max[first + r], run_sum[first + r], acc[first + r] = new

    def pick(half, lines):
        return jnp.where(half == 0, lines[0], lines[1])

    def fold_both(lines, part):
        def one(half, carry):
            fold(half, pick(half, lines), part)
            return carry

        lax.fori_loop(0, 2, one, 0)

    own = (xy, xy)
    for s in range(1, line):
        pass_line(s)
        if s == group - 1 or line == 2:
            start_bias(0)
            pass_near(s - 1)
            spread_bias(0)
            fold_both(own, own_part)
        elif s == line - 2:
            start_bias(1)
            start_bias(2)
            pass_near(s - 1)
            spread_bias(1)
            spread_bias(2)
            fold_both(near, own_part)
        else:
            pass_near(s - 1)
    start_bias(3)
    fold_both(own, 1 - own_part)
    pass_near(line - 1)
    spread_bias(3)
    fold_both(near, 1 - own_part)

    def late(unit, carry):
        half, stage = lax.rem(unit, 2), unit // 2
        line_at = jnp.where(stage < 2, pick(half, far), diag)
        part = jnp.where(lax.rem(stage, 2) == 0, own_part, 1 - own_part)
        for z_at in range(group):
            block = gath.at[line_at, part * group + z_at, pl.ds(half * quarter, quarter)]
            pltpu.make_async_copy(block, block, recv.at[half, line_at, part * group + z_at]).wait()
        fold(half, line_at, part)
        return carry

    lax.fori_loop(0, 7, late, 0)

    other_cols = pl.ds(pl.multiple_of((1 - core) * cols, cols), cols)

    def out_copy(half):
        return pltpu.make_async_remote_copy(
            src_ref=upd.at[pl.ds(half * quarter, quarter), other_cols, :],
            dst_ref=out_ref.at[pl.ds(core * half_rows + half * quarter, quarter)],
            send_sem=core_s.at[1 + half], recv_sem=core_r.at[1 + half],
            device_id={"col": sibling}, device_id_type=MESH,
        )

    for half in range(2):
        if half:
            late(7, 0)
        hiddens = []
        for r in range(half * quarter, (half + 1) * quarter):
            scale = 1.0 / run_sum[r]
            parts = []
            for h in range(HEADS):
                block = acc[r, h * width : (h + 1) * width] * scale[:, (h // 2) * per_pair : (h // 2 + 1) * per_pair]
                if h % 2:
                    block = pltpu.roll(block, cols2, 1)
                parts.append(block[:, :cols2])
            attended = jnp.concatenate(parts, axis=0)
            hiddens.append((gate[r] * attended).T.astype(BF16))
        update = dot(jnp.concatenate(hiddens, axis=0), wo_ref[...]).astype(BF16)
        upd[pl.ds(half * quarter, quarter)] = update.reshape(quarter, cols2, chan)
        out_copy(half).start()
        out_ref[pl.ds(core * half_rows + half * quarter, quarter)] = upd[
            pl.ds(half * quarter, quarter), own_cols, :
        ]

    for half in range(2):
        out_copy(half).wait()
        for z_at in range(line):
            pl.when((z + 1 < line) & (z >= z_at))(lambda: up(half, z_at).wait_send())
            pl.when((z > 0) & (z <= z_at))(lambda: down(half, z_at).wait_send())
            to_near(half, z_at).wait_send()
            to_far(half, 0, z_at).wait_send()
            to_far(half, 1, z_at).wait_send()
    swap_copy.wait_send()
    for at, (line_at, first) in enumerate(all_lines):
        bias_peers(line_at, first, lambda other: bias_copy(other, chip).wait_send())
        bias_swap(at).wait_send()


def solution(mesh):
    chips = mesh.shape["col"] // 2
    line = chips // 4

    def on_device(pair, w_query, w_kv, w_gate, w_out, pair_bias, lengths):
        rows, cols, chan = pair.shape
        half_rows, cols2 = rows // 2, 2 * cols
        quarter = half_rows // 2
        lanes = HEADS * cols2
        vmem = pl.BlockSpec(memory_space=pltpu.VMEM)
        dma = pltpu.SemaphoreType.DMA
        return pl.pallas_call(
            functools.partial(body, line),
            out_shape=jax.ShapeDtypeStruct(pair.shape, BF16),
            in_specs=[pl.BlockSpec(memory_space=pl.ANY)] * 6 + [pl.BlockSpec(memory_space=pltpu.SMEM)],
            out_specs=vmem,
            scratch_shapes=[
                pltpu.VMEM(pair.shape, BF16),
                pltpu.VMEM(pair_bias.shape, BF16),
                pltpu.VMEM(w_query.shape, BF16),
                pltpu.VMEM(w_kv.shape, BF16),
                pltpu.VMEM(w_gate.shape, BF16),
                pltpu.VMEM(w_out.shape, BF16),
                dma((6,)),
                pltpu.VMEM((4, line, half_rows, cols2, chan), BF16),
                pltpu.VMEM((half_rows, cols, chan), BF16),
                pltpu.VMEM((chips, cols, lanes), BF16),
                pltpu.VMEM((4, line, cols2, lanes), BF16),
                pltpu.VMEM((4, line, cols2, lanes), F32),
                pltpu.VMEM((half_rows, chan, lanes), BF16),
                pltpu.VMEM((half_rows, chan, cols2), F32),
                pltpu.VMEM((half_rows, chan, 2 * cols2), F32),
                pltpu.VMEM((half_rows, 1, lanes), F32),
                pltpu.VMEM((half_rows, 1, lanes), F32),
                pltpu.VMEM((half_rows, cols2, chan), BF16),
                pltpu.VMEM((chan, chan), BF16),
                dma((2, 4, line)),
                dma((2, 2, line)),
                dma((2, line)),
                dma((2, 2, line)),
                dma((chips,)),
                dma((chips,)),
                dma((7,)),
                dma((7,)),
            ],
            compiler_params=pltpu.CompilerParams(
                collective_id=0, has_side_effects=True
            ),
            cost_estimate=pl.CostEstimate(flops=3 * 10**9, bytes_accessed=10**6, transcendentals=2 * 10**6),
        )(pair, w_query, w_kv, w_gate, w_out, pair_bias, lengths)

    in_specs = (P("grp", "col", None), P(), P(), P(), P(), P("grp", "col", None), P("grp"))
    return jax.shard_map(
        on_device, mesh=mesh, in_specs=in_specs, out_specs=P("grp", "col", None), check_vma=False
    )
```

```python
import functools

import jax
import jax.numpy as jnp
from jax import lax
from jax.experimental import pallas as pl
from jax.experimental.pallas import tpu as pltpu
from jax.sharding import PartitionSpec as P

HEADS = 4
PEERS = 4
SIDES = 2
MESH = pl.DeviceIdType.MESH
F32 = jnp.float32
BF16 = jnp.bfloat16
LOG2E = 1.4426950408889634
NT = (((1,), (1,)), ((), ()))


def dot(lhs, rhs):
    return jnp.dot(lhs, rhs, preferred_element_type=F32)


def dot_nt(lhs, rhs):
    return lax.dot_general(lhs, rhs, NT, preferred_element_type=F32)


def transposed(weight):
    return weight.astype(F32).T.astype(BF16)


def body(
    line, pair_in, wq_in, wkv_in, wg_in, wo_in, bias_in, len_ref, out_ref,
    pair_ref, bias_ref, wq_ref, wkv_ref, wg_ref, wo_ref, load_sem,
    gath, swap, bsend, bgath, queries, gate, acc, run_max, run_sum, upd, wvt_ref,
    swap_s, swap_r, z_s, y_s, recv, bias_s, bias_r, share_s, share_r, out_s, out_r,
):
    rows, cols, chan = pair_ref.shape
    part_rows, cols4 = rows // PEERS, PEERS * cols
    half_rows = part_rows // 2
    width = chan // HEADS
    lanes = HEADS * cols4
    quads = SIDES * line

    me = lax.axis_index("col")
    place = lax.rem(me, PEERS)
    quad = me // PEERS
    z = quad // SIDES
    side = lax.rem(quad, SIDES)
    other_side = 1 - side

    def device(z_at, side_at):
        return {"col": (z_at * SIDES + side_at) * PEERS + place}

    def peer(k):
        return lax.rem(place + k, PEERS)

    def peer_device(k):
        return {"col": quad * PEERS + peer(k)}

    loads = [
        pltpu.make_async_copy(source, target, load_sem.at[at])
        for at, (source, target) in enumerate((
            (pair_in, pair_ref), (bias_in, bias_ref), (wq_in, wq_ref),
            (wkv_in, wkv_ref), (wg_in, wg_ref), (wo_in, wo_ref),
        ))
    ]
    for load in loads:
        load.start()

    barrier = pltpu.get_barrier_semaphore()

    def greet(k, carry):
        other = lax.rem(quad + k, quads)
        pl.semaphore_signal(barrier, inc=1, device_id={"col": other * PEERS + place}, device_id_type=MESH)
        return carry

    lax.fori_loop(1, quads, greet, 0)
    for k in range(1, PEERS):
        pl.semaphore_signal(barrier, inc=1, device_id=peer_device(k), device_id_type=MESH)

    loads[0].wait()
    values = pair_ref[...].astype(F32)
    centred = values - jnp.mean(values, axis=-1, keepdims=True)
    variance = jnp.mean(centred * centred, axis=-1, keepdims=True)
    swap[...] = (centred * lax.rsqrt(variance + 1e-05)).astype(BF16)

    pl.semaphore_wait(barrier, quads - 1 + PEERS - 1)

    def cols_of(place_at):
        return pl.ds(pl.multiple_of(place_at * cols, cols), cols)

    def swap_copy(k, from_place):
        return pltpu.make_async_remote_copy(
            src_ref=swap.at[pl.ds(peer(k) * part_rows, part_rows)],
            dst_ref=gath.at[side, z, :, cols_of(from_place), :],
            send_sem=swap_s.at[k], recv_sem=swap_r.at[from_place],
            device_id=peer_device(k), device_id_type=MESH,
        )

    for k in range(1, PEERS):
        swap_copy(k, place).start()
    gath[side, z, :, cols_of(place), :] = swap[pl.ds(place * part_rows, part_rows)]

    loads[1].wait()
    for at in range(quads):
        for h in range(HEADS):
            bsend[at, :, h * cols4 : (h + 1) * cols4] = bias_ref[h, :, at * cols4 : (at + 1) * cols4]
    bgath[side, z, cols_of(place), :] = bsend[quad]

    def share_copy(side_at, z_at, k, from_place):
        block = bgath.at[side_at, z_at, cols_of(from_place), :]
        return pltpu.make_async_remote_copy(
            src_ref=block, dst_ref=block,
            send_sem=share_s.at[side_at, z_at, k], recv_sem=share_r.at[side_at, z_at, from_place],
            device_id=peer_device(k), device_id_type=MESH,
        )

    def share(side_at, z_at):
        for k in range(1, PEERS):
            share_copy(side_at, z_at, k, place).start()

    for k in range(1, PEERS):
        swap_copy(k, peer(k)).wait_recv()

    def block_copy(half, side_at, z_at, target, send_sem):
        block = gath.at[side_at, z_at, pl.ds(half * half_rows, half_rows)]
        return pltpu.make_async_remote_copy(
            src_ref=block, dst_ref=block, send_sem=send_sem, recv_sem=recv.at[half, side_at, z_at],
            device_id=target, device_id_type=MESH,
        )

    def up(half, z_at):
        return block_copy(half, side, z_at, device(z + 1, side), z_s.at[half, 0, z_at])

    def down(half, z_at):
        return block_copy(half, side, z_at, device(z - 1, side), z_s.at[half, 1, z_at])

    def across(half, z_at):
        return block_copy(half, side, z_at, device(z, other_side), y_s.at[half, z_at])

    def arrived(half, side_at, z_at):
        block_copy(half, side_at, z_at, device(z, other_side), y_s.at[half, z_at]).wait_recv()

    def forward(half, z_at):
        pl.when((z + 1 < line) & (z_at <= z))(lambda: up(half, z_at).start())
        pl.when((z > 0) & (z_at >= z))(lambda: down(half, z_at).start())
        across(half, z_at).start()

    for half in range(2):
        forward(half, z)

    margin = jnp.minimum(z, line - 1 - z)

    def ranked(at):
        step = (at + 1) // 2
        close = jnp.where(lax.rem(at, 2) == 1, z + step, z - step)
        rest = jnp.where(z == margin, at, line - 1 - at)
        return jnp.where(at <= 2 * margin, close, rest)

    def bias_copy(side_to, z_to, side_from, z_from):
        return pltpu.make_async_remote_copy(
            src_ref=bsend.at[z_to * SIDES + side_to], dst_ref=bgath.at[side_from, z_from, cols_of(place), :],
            send_sem=bias_s.at[side_to, z_to], recv_sem=bias_r.at[side_from, z_from],
            device_id=device(z_to, side_to), device_id_type=MESH,
        )

    def send_bias(side_to, first):
        def one(at, carry):
            bias_copy(side_to, ranked(at), side, z).start()
            return carry

        lax.fori_loop(first, line, one, 0)

    share(side, z)
    send_bias(side, 1)
    send_bias(other_side, 0)

    for load in loads[2:]:
        load.wait()
    wqt = transposed(wq_ref[...])
    wgt = transposed(wg_ref[...])
    wvt_ref[...] = transposed(wkv_ref[:, chan:])
    head_of = lax.broadcasted_iota(jnp.int32, (chan, cols4), 0) // width
    own = gath[side, z].reshape(part_rows * cols4, chan)
    all_queries = (dot_nt(wqt, own) * width ** (-0.5)).astype(BF16).astype(F32)
    all_gates = jax.nn.sigmoid(dot_nt(wgt, own))
    for r in range(part_rows):
        span = slice(r * cols4, (r + 1) * cols4)
        gate[r] = all_gates[:, span]
        for h in range(HEADS):
            one_head = jnp.where(head_of == h, all_queries[:, span], 0.0)
            queries[r, :, h * cols4 : (h + 1) * cols4] = one_head.astype(BF16)

    run_max[...] = jnp.full_like(run_max, -1e30)
    run_sum[...] = jnp.zeros_like(run_sum)
    acc[...] = jnp.zeros_like(acc)
    limit = len_ref[0]

    def fold(side_at, z_at):
        for k in range(1, PEERS):
            share_copy(side_at, z_at, k, peer(k)).wait_recv()
        tiles = gath[side_at, z_at].reshape(part_rows * cols4, chan)
        olds = [(run_max[r], run_sum[r], acc[r]) for r in range(part_rows)]
        position = (z_at * SIDES + side_at) * cols4 + lax.broadcasted_iota(jnp.int32, (cols4, lanes), 0)
        mask = jnp.where(position < limit, 0.0, -1000000000.0)
        bias_tile = (bgath[side_at, z_at].astype(F32) + mask) * LOG2E
        all_keys = dot(tiles, wkv_ref[:, :chan]).astype(BF16)
        all_values = dot_nt(wvt_ref[...], tiles).astype(BF16)
        news = []
        for r, (old_max, old_sum, old_acc) in enumerate(olds):
            span = slice(r * cols4, (r + 1) * cols4)
            scores = dot(all_keys[span], queries[r]) * LOG2E + bias_tile
            new_max = jnp.maximum(old_max, jnp.max(scores, axis=0, keepdims=True))
            rescale = jnp.exp2(old_max - new_max)
            expon = jnp.exp2(scores - new_max)
            total = old_sum * rescale + jnp.sum(expon, axis=0, keepdims=True)
            weights = expon.astype(BF16)
            result = []
            for h in range(0, HEADS, 2):
                both = dot(
                    all_values[h * width : (h + 2) * width, span],
                    weights[:, h * cols4 : (h + 2) * cols4],
                )
                for which in range(2):
                    at = slice((h + which) * width, (h + which + 1) * width)
                    scale = rescale[:, (h + which) * cols4 : (h + which + 1) * cols4]
                    part = both[which * width : (which + 1) * width, which * cols4 : (which + 1) * cols4]
                    result.append(old_acc[at] * scale + part)
            news.append((new_max, total, jnp.concatenate(result, axis=0)))
        for r, new in enumerate(news):
            run_max[r], run_sum[r], acc[r] = new

    def take_bias(side_at, z_at):
        bias_copy(side_at, z_at, side_at, z_at).wait_recv()
        share(side_at, z_at)

    def advance(at, carry):
        z_at = ranked(at)
        for half in range(2):
            arrived(half, side, z_at)
            forward(half, z_at)
        take_bias(side, z_at)
        take_bias(other_side, ranked(at - 1))
        fold(side, ranked(at - 1))
        return carry

    lax.fori_loop(1, line, advance, 0)
    take_bias(other_side, ranked(line - 1))

    def late(at, carry):
        side_at = jnp.where(at == 0, side, other_side)
        z_at = ranked(jnp.where(at == 0, line - 1, at - 1))

        def wait_blocks():
            for half in range(2):
                arrived(half, other_side, z_at)

        pl.when(at > 0)(wait_blocks)
        fold(side_at, z_at)
        return carry

    lax.fori_loop(0, line + 1, late, 0)

    hiddens = []
    for r in range(part_rows):
        scale = 1.0 / run_sum[r]
        attended = jnp.concatenate(
            [
                acc[r, h * width : (h + 1) * width] * scale[:, h * cols4 : (h + 1) * cols4]
                for h in range(HEADS)
            ],
            axis=0,
        )
        hiddens.append((gate[r] * attended).T.astype(BF16))
    update = dot(jnp.concatenate(hiddens, axis=0), wo_ref[...]).astype(BF16)
    upd[...] = update.reshape(part_rows, cols4, chan)

    def out_copy(k, from_place):
        return pltpu.make_async_remote_copy(
            src_ref=upd.at[:, cols_of(peer(k)), :],
            dst_ref=out_ref.at[pl.ds(from_place * part_rows, part_rows)],
            send_sem=out_s.at[k], recv_sem=out_r.at[from_place],
            device_id=peer_device(k), device_id_type=MESH,
        )

    for k in range(1, PEERS):
        out_copy(k, place).start()
    out_ref[pl.ds(place * part_rows, part_rows)] = upd[:, cols_of(place), :]

    for k in range(1, PEERS):
        swap_copy(k, place).wait_send()
    for half in range(2):
        for z_at in range(line):
            pl.when((z + 1 < line) & (z_at <= z))(lambda: up(half, z_at).wait_send())
            pl.when((z > 0) & (z_at >= z))(lambda: down(half, z_at).wait_send())
            across(half, z_at).wait_send()

    def drain(at, carry):
        side_at, z_at = at // line, lax.rem(at, line)
        pl.when((side_at != side) | (z_at != z))(lambda: bias_copy(side_at, z_at, side, z).wait_send())
        for k in range(1, PEERS):
            share_copy(side_at, z_at, k, place).wait_send()
        return carry

    lax.fori_loop(0, quads, drain, 0)
    for k in range(1, PEERS):
        out_copy(k, place).wait_send()
        out_copy(k, peer(k)).wait_recv()


def solution(mesh):
    quads = mesh.shape["col"] // PEERS
    line = quads // SIDES

    def on_device(pair, w_query, w_kv, w_gate, w_out, pair_bias, lengths):
        rows, cols, chan = pair.shape
        part_rows, cols4 = rows // PEERS, PEERS * cols
        lanes = HEADS * cols4
        vmem = pl.BlockSpec(memory_space=pltpu.VMEM)
        dma = pltpu.SemaphoreType.DMA
        return pl.pallas_call(
            functools.partial(body, line),
            out_shape=jax.ShapeDtypeStruct(pair.shape, BF16),
            in_specs=[pl.BlockSpec(memory_space=pl.ANY)] * 6 + [pl.BlockSpec(memory_space=pltpu.SMEM)],
            out_specs=vmem,
            scratch_shapes=[
                pltpu.VMEM(pair.shape, BF16),
                pltpu.VMEM(pair_bias.shape, BF16),
                pltpu.VMEM(w_query.shape, BF16),
                pltpu.VMEM(w_kv.shape, BF16),
                pltpu.VMEM(w_gate.shape, BF16),
                pltpu.VMEM(w_out.shape, BF16),
                dma((6,)),
                pltpu.VMEM((SIDES, line, part_rows, cols4, chan), BF16),
                pltpu.VMEM((rows, cols, chan), BF16),
                pltpu.VMEM((quads, cols, lanes), BF16),
                pltpu.VMEM((SIDES, line, cols4, lanes), BF16),
                pltpu.VMEM((part_rows, chan, lanes), BF16),
                pltpu.VMEM((part_rows, chan, cols4), F32),
                pltpu.VMEM((part_rows, chan, cols4), F32),
                pltpu.VMEM((part_rows, 1, lanes), F32),
                pltpu.VMEM((part_rows, 1, lanes), F32),
                pltpu.VMEM((part_rows, cols4, chan), BF16),
                pltpu.VMEM((chan, chan), BF16),
                dma((PEERS,)),
                dma((PEERS,)),
                dma((2, 2, line)),
                dma((2, line)),
                dma((2, SIDES, line)),
                dma((SIDES, line)),
                dma((SIDES, line)),
                dma((SIDES, line, PEERS)),
                dma((SIDES, line, PEERS)),
                dma((PEERS,)),
                dma((PEERS,)),
            ],
            compiler_params=pltpu.CompilerParams(collective_id=0, has_side_effects=True),
            cost_estimate=pl.CostEstimate(flops=3 * 10**9, bytes_accessed=10**6, transcendentals=2 * 10**6),
        )(pair, w_query, w_kv, w_gate, w_out, pair_bias, lengths)

    in_specs = (P("grp", "col", None), P(), P(), P(), P(), P("grp", "col", None), P("grp"))
    return jax.shard_map(
        on_device, mesh=mesh, in_specs=in_specs, out_specs=P("grp", "col", None), check_vma=False
    )
```

```python
import functools

import jax
import jax.numpy as jnp
from jax import lax
from jax.experimental import pallas as pl
from jax.experimental.pallas import tpu as pltpu
from jax.sharding import PartitionSpec as P

HEADS = 4
PEERS = 4
SIDES = 2
MESH = pl.DeviceIdType.MESH
F32 = jnp.float32
BF16 = jnp.bfloat16
LOG2E = 1.4426950408889634
NT = (((1,), (1,)), ((), ()))


def dot(lhs, rhs):
    return jnp.dot(lhs, rhs, preferred_element_type=F32)


def dot_nt(lhs, rhs):
    return lax.dot_general(lhs, rhs, NT, preferred_element_type=F32)


def transposed(weight):
    return weight.astype(F32).T.astype(BF16)


def body(
    line, pair_in, wq_in, wkv_in, wg_in, wo_in, bias_in, len_ref, out_ref,
    pair_ref, bias_ref, wq_ref, wkv_ref, wg_ref, wo_ref, load_sem,
    gath, swap, bsend, bgath, queries, gate, acc, run_max, run_sum, upd, wvt_ref,
    swap_s, swap_r, z_s, y_s, recv, bias_s, bias_r, share_s, share_r, out_s, out_r,
):
    rows, cols, chan = pair_ref.shape
    part_rows, cols4 = rows // PEERS, PEERS * cols
    half_rows = part_rows // 2
    width = chan // HEADS
    lanes = HEADS * cols4
    quads = SIDES * line

    me = lax.axis_index("col")
    place = lax.rem(me, PEERS)
    quad = me // PEERS
    z = quad // SIDES
    side = lax.rem(quad, SIDES)
    other_side = 1 - side

    def device(z_at, side_at):
        return {"col": (z_at * SIDES + side_at) * PEERS + place}

    def peer(k):
        return lax.rem(place + k, PEERS)

    def peer_device(k):
        return {"col": quad * PEERS + peer(k)}

    loads = [
        pltpu.make_async_copy(source, target, load_sem.at[at])
        for at, (source, target) in enumerate((
            (pair_in, pair_ref), (bias_in, bias_ref), (wq_in, wq_ref),
            (wkv_in, wkv_ref), (wg_in, wg_ref), (wo_in, wo_ref),
        ))
    ]
    for load in loads:
        load.start()

    barrier = pltpu.get_barrier_semaphore()

    def greet(k, carry):
        other = lax.rem(quad + k, quads)
        pl.semaphore_signal(barrier, inc=1, device_id={"col": other * PEERS + place}, device_id_type=MESH)
        return carry

    lax.fori_loop(1, quads, greet, 0)
    for k in range(1, PEERS):
        pl.semaphore_signal(barrier, inc=1, device_id=peer_device(k), device_id_type=MESH)

    loads[0].wait()
    values = pair_ref[...].astype(F32)
    centred = values - jnp.mean(values, axis=-1, keepdims=True)
    variance = jnp.mean(centred * centred, axis=-1, keepdims=True)
    swap[...] = (centred * lax.rsqrt(variance + 1e-05)).astype(BF16)

    pl.semaphore_wait(barrier, quads - 1 + PEERS - 1)

    def cols_of(place_at):
        return pl.ds(pl.multiple_of(place_at * cols, cols), cols)

    def swap_copy(k, from_place):
        return pltpu.make_async_remote_copy(
            src_ref=swap.at[pl.ds(peer(k) * part_rows, part_rows)],
            dst_ref=gath.at[side, z, :, cols_of(from_place), :],
            send_sem=swap_s.at[k], recv_sem=swap_r.at[from_place],
            device_id=peer_device(k), device_id_type=MESH,
        )

    for k in range(1, PEERS):
        swap_copy(k, place).start()
    gath[side, z, :, cols_of(place), :] = swap[pl.ds(place * part_rows, part_rows)]

    loads[1].wait()
    for at in range(quads):
        for h in range(HEADS):
            bsend[at, :, h * cols4 : (h + 1) * cols4] = bias_ref[h, :, at * cols4 : (at + 1) * cols4]
    bgath[side, z, cols_of(place), :] = bsend[quad]

    def share_copy(side_at, z_at, k, from_place):
        block = bgath.at[side_at, z_at, cols_of(from_place), :]
        return pltpu.make_async_remote_copy(
            src_ref=block, dst_ref=block,
            send_sem=share_s.at[side_at, z_at, k], recv_sem=share_r.at[side_at, z_at, from_place],
            device_id=peer_device(k), device_id_type=MESH,
        )

    def share(side_at, z_at):
        for k in range(1, PEERS):
            share_copy(side_at, z_at, k, place).start()

    for k in range(1, PEERS):
        swap_copy(k, peer(k)).wait_recv()

    def block_copy(half, side_at, z_at, target, send_sem):
        block = gath.at[side_at, z_at, pl.ds(half * half_rows, half_rows)]
        return pltpu.make_async_remote_copy(
            src_ref=block, dst_ref=block, send_sem=send_sem, recv_sem=recv.at[half, side_at, z_at],
            device_id=target, device_id_type=MESH,
        )

    def up(half, z_at):
        return block_copy(half, side, z_at, device(z + 1, side), z_s.at[half, 0, z_at])

    def down(half, z_at):
        return block_copy(half, side, z_at, device(z - 1, side), z_s.at[half, 1, z_at])

    def across(half, z_at):
        return block_copy(half, side, z_at, device(z, other_side), y_s.at[half, z_at])

    def arrived(half, side_at, z_at):
        block_copy(half, side_at, z_at, device(z, other_side), y_s.at[half, z_at]).wait_recv()

    def forward(half, z_at):
        pl.when((z + 1 < line) & (z_at <= z))(lambda: up(half, z_at).start())
        pl.when((z > 0) & (z_at >= z))(lambda: down(half, z_at).start())
        across(half, z_at).start()

    for half in range(2):
        forward(half, z)

    margin = jnp.minimum(z, line - 1 - z)

    def ranked(at):
        step = (at + 1) // 2
        close = jnp.where(lax.rem(at, 2) == 1, z + step, z - step)
        rest = jnp.where(z == margin, at, line - 1 - at)
        return jnp.where(at <= 2 * margin, close, rest)

    def bias_copy(side_to, z_to, side_from, z_from):
        return pltpu.make_async_remote_copy(
            src_ref=bsend.at[z_to * SIDES + side_to], dst_ref=bgath.at[side_from, z_from, cols_of(place), :],
            send_sem=bias_s.at[side_to, z_to], recv_sem=bias_r.at[side_from, z_from],
            device_id=device(z_to, side_to), device_id_type=MESH,
        )

    def send_bias(side_to, first):
        def one(at, carry):
            bias_copy(side_to, ranked(at), side, z).start()
            return carry

        lax.fori_loop(first, line, one, 0)

    share(side, z)
    send_bias(side, 1)
    send_bias(other_side, 0)

    for load in loads[2:]:
        load.wait()
    wqt = transposed(wq_ref[...])
    wgt = transposed(wg_ref[...])
    wvt_ref[...] = transposed(wkv_ref[:, chan:])
    head_of = lax.broadcasted_iota(jnp.int32, (chan, cols4), 0) // width
    own = gath[side, z].reshape(part_rows * cols4, chan)
    all_queries = (dot_nt(wqt, own) * width ** (-0.5)).astype(BF16).astype(F32)
    all_gates = jax.nn.sigmoid(dot_nt(wgt, own))
    for r in range(part_rows):
        span = slice(r * cols4, (r + 1) * cols4)
        gate[r] = all_gates[:, span]
        for h in range(HEADS):
            one_head = jnp.where(head_of == h, all_queries[:, span], 0.0)
            queries[r, :, h * cols4 : (h + 1) * cols4] = one_head.astype(BF16)

    run_max[...] = jnp.full_like(run_max, -1e30)
    run_sum[...] = jnp.zeros_like(run_sum)
    acc[...] = jnp.zeros_like(acc)
    limit = len_ref[0]

    def fold(side_at, z_at):
        for k in range(1, PEERS):
            share_copy(side_at, z_at, k, peer(k)).wait_recv()
        tiles = gath[side_at, z_at].reshape(part_rows * cols4, chan)
        olds = [(run_max[r], run_sum[r], acc[r]) for r in range(part_rows)]
        position = (z_at * SIDES + side_at) * cols4 + lax.broadcasted_iota(jnp.int32, (cols4, lanes), 0)
        mask = jnp.where(position < limit, 0.0, -1000000000.0)
        bias_tile = (bgath[side_at, z_at].astype(F32) + mask) * LOG2E
        all_keys = dot(tiles, wkv_ref[:, :chan]).astype(BF16)
        all_values = dot_nt(wvt_ref[...], tiles).astype(BF16)
        news = []
        for r, (old_max, old_sum, old_acc) in enumerate(olds):
            span = slice(r * cols4, (r + 1) * cols4)
            scores = dot(all_keys[span], queries[r]) * LOG2E + bias_tile
            new_max = jnp.maximum(old_max, jnp.max(scores, axis=0, keepdims=True))
            rescale = jnp.exp2(old_max - new_max)
            expon = jnp.exp2(scores - new_max)
            total = old_sum * rescale + jnp.sum(expon, axis=0, keepdims=True)
            weights = expon.astype(BF16)
            result = []
            for h in range(0, HEADS, 2):
                both = dot(
                    all_values[h * width : (h + 2) * width, span],
                    weights[:, h * cols4 : (h + 2) * cols4],
                )
                for which in range(2):
                    at = slice((h + which) * width, (h + which + 1) * width)
                    scale = rescale[:, (h + which) * cols4 : (h + which + 1) * cols4]
                    part = both[which * width : (which + 1) * width, which * cols4 : (which + 1) * cols4]
                    result.append(old_acc[at] * scale + part)
            news.append((new_max, total, jnp.concatenate(result, axis=0)))
        for r, new in enumerate(news):
            run_max[r], run_sum[r], acc[r] = new

    def take_bias(side_at, z_at):
        bias_copy(side_at, z_at, side_at, z_at).wait_recv()
        share(side_at, z_at)

    def advance(at, carry):
        z_at = ranked(at)
        for half in range(2):
            arrived(half, side, z_at)
            forward(half, z_at)
        take_bias(side, z_at)
        take_bias(other_side, ranked(at - 1))
        fold(side, ranked(at - 1))

        def cross():
            for half in range(2):
                arrived(half, other_side, ranked(at - 2))
            fold(other_side, ranked(at - 2))

        pl.when(at > 1)(cross)
        return carry

    lax.fori_loop(1, line, advance, 0)
    take_bias(other_side, ranked(line - 1))

    def late(at, carry):
        side_at = jnp.where(at == 0, side, other_side)
        z_at = ranked(jnp.where(at == 0, line - 1, line - 3 + at))

        def wait_blocks():
            for half in range(2):
                arrived(half, other_side, z_at)

        pl.when(at > 0)(wait_blocks)
        fold(side_at, z_at)
        return carry

    lax.fori_loop(0, 3, late, 0)

    hiddens = []
    for r in range(part_rows):
        scale = 1.0 / run_sum[r]
        attended = jnp.concatenate(
            [
                acc[r, h * width : (h + 1) * width] * scale[:, h * cols4 : (h + 1) * cols4]
                for h in range(HEADS)
            ],
            axis=0,
        )
        hiddens.append((gate[r] * attended).T.astype(BF16))
    update = dot(jnp.concatenate(hiddens, axis=0), wo_ref[...]).astype(BF16)
    upd[...] = update.reshape(part_rows, cols4, chan)

    def out_copy(k, from_place):
        return pltpu.make_async_remote_copy(
            src_ref=upd.at[:, cols_of(peer(k)), :],
            dst_ref=out_ref.at[pl.ds(from_place * part_rows, part_rows)],
            send_sem=out_s.at[k], recv_sem=out_r.at[from_place],
            device_id=peer_device(k), device_id_type=MESH,
        )

    for k in range(1, PEERS):
        out_copy(k, place).start()
    out_ref[pl.ds(place * part_rows, part_rows)] = upd[:, cols_of(place), :]

    for k in range(1, PEERS):
        swap_copy(k, place).wait_send()
    for half in range(2):
        for z_at in range(line):
            pl.when((z + 1 < line) & (z_at <= z))(lambda: up(half, z_at).wait_send())
            pl.when((z > 0) & (z_at >= z))(lambda: down(half, z_at).wait_send())
            across(half, z_at).wait_send()

    def drain(at, carry):
        side_at, z_at = at // line, lax.rem(at, line)
        pl.when((side_at != side) | (z_at != z))(lambda: bias_copy(side_at, z_at, side, z).wait_send())
        for k in range(1, PEERS):
            share_copy(side_at, z_at, k, place).wait_send()
        return carry

    lax.fori_loop(0, quads, drain, 0)
    for k in range(1, PEERS):
        out_copy(k, place).wait_send()
        out_copy(k, peer(k)).wait_recv()


def solution(mesh):
    quads = mesh.shape["col"] // PEERS
    line = quads // SIDES

    def on_device(pair, w_query, w_kv, w_gate, w_out, pair_bias, lengths):
        rows, cols, chan = pair.shape
        part_rows, cols4 = rows // PEERS, PEERS * cols
        lanes = HEADS * cols4
        vmem = pl.BlockSpec(memory_space=pltpu.VMEM)
        dma = pltpu.SemaphoreType.DMA
        return pl.pallas_call(
            functools.partial(body, line),
            out_shape=jax.ShapeDtypeStruct(pair.shape, BF16),
            in_specs=[pl.BlockSpec(memory_space=pl.ANY)] * 6 + [pl.BlockSpec(memory_space=pltpu.SMEM)],
            out_specs=vmem,
            scratch_shapes=[
                pltpu.VMEM(pair.shape, BF16),
                pltpu.VMEM(pair_bias.shape, BF16),
                pltpu.VMEM(w_query.shape, BF16),
                pltpu.VMEM(w_kv.shape, BF16),
                pltpu.VMEM(w_gate.shape, BF16),
                pltpu.VMEM(w_out.shape, BF16),
                dma((6,)),
                pltpu.VMEM((SIDES, line, part_rows, cols4, chan), BF16),
                pltpu.VMEM((rows, cols, chan), BF16),
                pltpu.VMEM((quads, cols, lanes), BF16),
                pltpu.VMEM((SIDES, line, cols4, lanes), BF16),
                pltpu.VMEM((part_rows, chan, lanes), BF16),
                pltpu.VMEM((part_rows, chan, cols4), F32),
                pltpu.VMEM((part_rows, chan, cols4), F32),
                pltpu.VMEM((part_rows, 1, lanes), F32),
                pltpu.VMEM((part_rows, 1, lanes), F32),
                pltpu.VMEM((part_rows, cols4, chan), BF16),
                pltpu.VMEM((chan, chan), BF16),
                dma((PEERS,)),
                dma((PEERS,)),
                dma((2, 2, line)),
                dma((2, line)),
                dma((2, SIDES, line)),
                dma((SIDES, line)),
                dma((SIDES, line)),
                dma((SIDES, line, PEERS)),
                dma((SIDES, line, PEERS)),
                dma((PEERS,)),
                dma((PEERS,)),
            ],
            compiler_params=pltpu.CompilerParams(collective_id=0, has_side_effects=True),
            cost_estimate=pl.CostEstimate(flops=3 * 10**9, bytes_accessed=10**6, transcendentals=2 * 10**6),
        )(pair, w_query, w_kv, w_gate, w_out, pair_bias, lengths)

    in_specs = (P("grp", "col", None), P(), P(), P(), P(), P("grp", "col", None), P("grp"))
    return jax.shard_map(
        on_device, mesh=mesh, in_specs=in_specs, out_specs=P("grp", "col", None), check_vma=False
    )
```

```python
import functools

import jax
import jax.numpy as jnp
from jax import lax
from jax.experimental import pallas as pl
from jax.experimental.pallas import tpu as pltpu
from jax.sharding import PartitionSpec as P

HEADS = 4
PEERS = 4
SIDES = 2
MESH = pl.DeviceIdType.MESH
F32 = jnp.float32
BF16 = jnp.bfloat16
LOG2E = 1.4426950408889634
NT = (((1,), (1,)), ((), ()))


def dot(lhs, rhs):
    return jnp.dot(lhs, rhs, preferred_element_type=F32)


def dot_nt(lhs, rhs):
    return lax.dot_general(lhs, rhs, NT, preferred_element_type=F32)


def transposed(weight):
    return weight.astype(F32).T.astype(BF16)


def body(
    line, pair_in, wq_in, wkv_in, wg_in, wo_in, bias_in, len_ref, out_ref,
    pair_ref, bias_ref, wq_ref, wkv_ref, wg_ref, wo_ref, load_sem,
    gath, swap, bsend, bgath, queries, gate, acc, run_max, run_sum, upd, wvt_ref,
    swap_s, swap_r, z_s, y_s, recv, bias_s, bias_r, share_s, share_r, out_s, out_r,
):
    rows, cols, chan = pair_ref.shape
    part_rows, cols4 = rows // PEERS, PEERS * cols
    half_rows = part_rows // 2
    width = chan // HEADS
    lanes = HEADS * cols4
    quads = SIDES * line

    me = lax.axis_index("col")
    place = lax.rem(me, PEERS)
    quad = me // PEERS
    z = quad // SIDES
    side = lax.rem(quad, SIDES)
    other_side = 1 - side

    def device(z_at, side_at):
        return {"col": (z_at * SIDES + side_at) * PEERS + place}

    def peer(k):
        return lax.rem(place + k, PEERS)

    def peer_device(k):
        return {"col": quad * PEERS + peer(k)}

    loads = [
        pltpu.make_async_copy(source, target, load_sem.at[at])
        for at, (source, target) in enumerate((
            (pair_in, pair_ref), (bias_in, bias_ref), (wq_in, wq_ref),
            (wkv_in, wkv_ref), (wg_in, wg_ref), (wo_in, wo_ref),
        ))
    ]
    for load in loads:
        load.start()

    barrier = pltpu.get_barrier_semaphore()

    def greet(k, carry):
        other = lax.rem(quad + k, quads)
        pl.semaphore_signal(barrier, inc=1, device_id={"col": other * PEERS + place}, device_id_type=MESH)
        return carry

    lax.fori_loop(1, quads, greet, 0)
    for k in range(1, PEERS):
        pl.semaphore_signal(barrier, inc=1, device_id=peer_device(k), device_id_type=MESH)

    loads[0].wait()
    values = pair_ref[...].astype(F32)
    centred = values - jnp.mean(values, axis=-1, keepdims=True)
    variance = jnp.mean(centred * centred, axis=-1, keepdims=True)
    swap[...] = (centred * lax.rsqrt(variance + 1e-05)).astype(BF16)

    pl.semaphore_wait(barrier, quads - 1 + PEERS - 1)

    def cols_of(place_at):
        return pl.ds(pl.multiple_of(place_at * cols, cols), cols)

    def swap_copy(k, from_place):
        return pltpu.make_async_remote_copy(
            src_ref=swap.at[pl.ds(peer(k) * part_rows, part_rows)],
            dst_ref=gath.at[side, z, :, cols_of(from_place), :],
            send_sem=swap_s.at[k], recv_sem=swap_r.at[from_place],
            device_id=peer_device(k), device_id_type=MESH,
        )

    for k in range(1, PEERS):
        swap_copy(k, place).start()
    gath[side, z, :, cols_of(place), :] = swap[pl.ds(place * part_rows, part_rows)]

    loads[1].wait()
    for at in range(quads):
        for h in range(HEADS):
            bsend[at, :, h * cols4 : (h + 1) * cols4] = bias_ref[h, :, at * cols4 : (at + 1) * cols4]
    bgath[side, z, cols_of(place), :] = bsend[quad]

    def share_copy(side_at, z_at, k, from_place):
        block = bgath.at[side_at, z_at, cols_of(from_place), :]
        return pltpu.make_async_remote_copy(
            src_ref=block, dst_ref=block,
            send_sem=share_s.at[side_at, z_at, k], recv_sem=share_r.at[side_at, z_at, from_place],
            device_id=peer_device(k), device_id_type=MESH,
        )

    def share(side_at, z_at):
        for k in range(1, PEERS):
            share_copy(side_at, z_at, k, place).start()

    for k in range(1, PEERS):
        swap_copy(k, peer(k)).wait_recv()

    def block_copy(half, side_at, z_at, target, send_sem):
        block = gath.at[side_at, z_at, pl.ds(half * half_rows, half_rows)]
        return pltpu.make_async_remote_copy(
            src_ref=block, dst_ref=block, send_sem=send_sem, recv_sem=recv.at[half, side_at, z_at],
            device_id=target, device_id_type=MESH,
        )

    def up(half, z_at):
        return block_copy(half, side, z_at, device(z + 1, side), z_s.at[half, 0, z_at])

    def down(half, z_at):
        return block_copy(half, side, z_at, device(z - 1, side), z_s.at[half, 1, z_at])

    def across(half, z_at):
        return block_copy(half, side, z_at, device(z, other_side), y_s.at[half, z_at])

    def arrived(half, side_at, z_at):
        block_copy(half, side_at, z_at, device(z, other_side), y_s.at[half, z_at]).wait_recv()

    def forward(half, z_at):
        pl.when((z + 1 < line) & (z_at <= z))(lambda: up(half, z_at).start())
        pl.when((z > 0) & (z_at >= z))(lambda: down(half, z_at).start())
        across(half, z_at).start()

    for half in range(2):
        forward(half, z)

    group = line // 2
    near_part = z // group
    inside = z - near_part * group
    margin = jnp.minimum(inside, group - 1 - inside)

    def ranked(at):
        step = (at + 1) // 2
        close = jnp.where(lax.rem(at, 2) == 1, inside + step, inside - step)
        rest = jnp.where(inside == margin, at, group - 1 - at)
        near = near_part * group + jnp.where(at <= 2 * margin, close, rest)
        far = jnp.where(near_part == 0, at, line - 1 - at)
        return jnp.where(at < group, near, far)

    def bias_copy(side_to, z_to, side_from, z_from):
        return pltpu.make_async_remote_copy(
            src_ref=bsend.at[z_to * SIDES + side_to], dst_ref=bgath.at[side_from, z_from, cols_of(place), :],
            send_sem=bias_s.at[side_to, z_to], recv_sem=bias_r.at[side_from, z_from],
            device_id=device(z_to, side_to), device_id_type=MESH,
        )

    def send_bias(side_to, first):
        def one(at, carry):
            bias_copy(side_to, ranked(at), side, z).start()
            return carry

        lax.fori_loop(first, line, one, 0)

    share(side, z)
    send_bias(side, 1)
    send_bias(other_side, 0)

    for load in loads[2:]:
        load.wait()
    wqt = transposed(wq_ref[...])
    wgt = transposed(wg_ref[...])
    wvt_ref[...] = transposed(wkv_ref[:, chan:])
    head_of = lax.broadcasted_iota(jnp.int32, (chan, cols4), 0) // width
    own = gath[side, z].reshape(part_rows * cols4, chan)
    all_queries = (dot_nt(wqt, own) * width ** (-0.5)).astype(BF16).astype(F32)
    all_gates = jax.nn.sigmoid(dot_nt(wgt, own))
    for r in range(part_rows):
        span = slice(r * cols4, (r + 1) * cols4)
        gate[r] = all_gates[:, span]
        for h in range(HEADS):
            one_head = jnp.where(head_of == h, all_queries[:, span], 0.0)
            queries[r, :, h * cols4 : (h + 1) * cols4] = one_head.astype(BF16)

    run_max[...] = jnp.full_like(run_max, -1e30)
    run_sum[...] = jnp.zeros_like(run_sum)
    acc[...] = jnp.zeros_like(acc)
    limit = len_ref[0]

    keys = 2 * cols4

    def fold(side_at, first):
        z_at = pl.ds(first, 2)
        for block in range(2):
            for k in range(1, PEERS):
                share_copy(side_at, first + block, k, peer(k)).wait_recv()
        tiles = jnp.concatenate(
            [gath[side_at, z_at, r].reshape(keys, chan) for r in range(part_rows)], axis=0
        )
        position = lax.broadcasted_iota(jnp.int32, (2, cols4, lanes), 1)
        position = position + lax.broadcasted_iota(jnp.int32, (2, cols4, lanes), 0) * SIDES * cols4
        mask = jnp.where(position < limit - (first * SIDES + side_at) * cols4, 0.0, -1000000000.0)
        bias_tile = ((bgath[side_at, z_at].astype(F32) + mask) * LOG2E).reshape(keys, lanes)
        olds = [(run_max[r], run_sum[r], acc[r]) for r in range(part_rows)]
        all_keys = dot(tiles, wkv_ref[:, :chan]).astype(BF16)
        all_values = dot_nt(wvt_ref[...], tiles).astype(BF16)
        news = []
        for r, (old_max, old_sum, old_acc) in enumerate(olds):
            span = slice(r * keys, (r + 1) * keys)
            scores = dot(all_keys[span], queries[r]) * LOG2E + bias_tile
            new_max = jnp.maximum(old_max, jnp.max(scores, axis=0, keepdims=True))
            rescale = jnp.exp2(old_max - new_max)
            expon = jnp.exp2(scores - new_max)
            total = old_sum * rescale + jnp.sum(expon, axis=0, keepdims=True)
            weights = expon.astype(BF16)
            result = []
            for h in range(0, HEADS, 2):
                both = dot(
                    all_values[h * width : (h + 2) * width, span],
                    weights[:, h * cols4 : (h + 2) * cols4],
                )
                for which in range(2):
                    at = slice((h + which) * width, (h + which + 1) * width)
                    scale = rescale[:, (h + which) * cols4 : (h + which + 1) * cols4]
                    part = both[which * width : (which + 1) * width, which * cols4 : (which + 1) * cols4]
                    result.append(old_acc[at] * scale + part)
            news.append((new_max, total, jnp.concatenate(result, axis=0)))
        for r, new in enumerate(news):
            run_max[r], run_sum[r], acc[r] = new

    def take_bias(side_at, z_at):
        bias_copy(side_at, z_at, side_at, z_at).wait_recv()
        share(side_at, z_at)

    def fold_half(side_at, part):
        def one(at, carry):
            fold(side_at, part * group + 2 * at)
            return carry

        lax.fori_loop(0, group // 2, one, 0)

    def fold_other(part):
        def one(at, carry):
            for half in range(2):
                arrived(half, other_side, part * group + at)
            return carry

        lax.fori_loop(0, group, one, 0)
        fold_half(other_side, part)

    def advance(at, carry):
        z_at = ranked(at)
        for half in range(2):
            arrived(half, side, z_at)
            forward(half, z_at)
        take_bias(side, z_at)
        take_bias(other_side, ranked(at - 1))
        pl.when(at == group - 1)(lambda: fold_half(side, near_part))
        pl.when(at == line - 2)(lambda: fold_other(near_part))
        return carry

    lax.fori_loop(1, line, advance, 0)
    take_bias(other_side, ranked(line - 1))
    fold_half(side, 1 - near_part)
    fold_other(1 - near_part)

    hiddens = []
    for r in range(part_rows):
        scale = 1.0 / run_sum[r]
        attended = jnp.concatenate(
            [
                acc[r, h * width : (h + 1) * width] * scale[:, h * cols4 : (h + 1) * cols4]
                for h in range(HEADS)
            ],
            axis=0,
        )
        hiddens.append((gate[r] * attended).T.astype(BF16))
    update = dot(jnp.concatenate(hiddens, axis=0), wo_ref[...]).astype(BF16)
    upd[...] = update.reshape(part_rows, cols4, chan)

    def out_copy(k, from_place):
        return pltpu.make_async_remote_copy(
            src_ref=upd.at[:, cols_of(peer(k)), :],
            dst_ref=out_ref.at[pl.ds(from_place * part_rows, part_rows)],
            send_sem=out_s.at[k], recv_sem=out_r.at[from_place],
            device_id=peer_device(k), device_id_type=MESH,
        )

    for k in range(1, PEERS):
        out_copy(k, place).start()
    out_ref[pl.ds(place * part_rows, part_rows)] = upd[:, cols_of(place), :]

    for k in range(1, PEERS):
        swap_copy(k, place).wait_send()
    for half in range(2):
        for z_at in range(line):
            pl.when((z + 1 < line) & (z_at <= z))(lambda: up(half, z_at).wait_send())
            pl.when((z > 0) & (z_at >= z))(lambda: down(half, z_at).wait_send())
            across(half, z_at).wait_send()

    def drain(at, carry):
        side_at, z_at = at // line, lax.rem(at, line)
        pl.when((side_at != side) | (z_at != z))(lambda: bias_copy(side_at, z_at, side, z).wait_send())
        for k in range(1, PEERS):
            share_copy(side_at, z_at, k, place).wait_send()
        return carry

    lax.fori_loop(0, quads, drain, 0)
    for k in range(1, PEERS):
        out_copy(k, place).wait_send()
        out_copy(k, peer(k)).wait_recv()


def solution(mesh):
    quads = mesh.shape["col"] // PEERS
    line = quads // SIDES

    def on_device(pair, w_query, w_kv, w_gate, w_out, pair_bias, lengths):
        rows, cols, chan = pair.shape
        part_rows, cols4 = rows // PEERS, PEERS * cols
        lanes = HEADS * cols4
        vmem = pl.BlockSpec(memory_space=pltpu.VMEM)
        dma = pltpu.SemaphoreType.DMA
        return pl.pallas_call(
            functools.partial(body, line),
            out_shape=jax.ShapeDtypeStruct(pair.shape, BF16),
            in_specs=[pl.BlockSpec(memory_space=pl.ANY)] * 6 + [pl.BlockSpec(memory_space=pltpu.SMEM)],
            out_specs=vmem,
            scratch_shapes=[
                pltpu.VMEM(pair.shape, BF16),
                pltpu.VMEM(pair_bias.shape, BF16),
                pltpu.VMEM(w_query.shape, BF16),
                pltpu.VMEM(w_kv.shape, BF16),
                pltpu.VMEM(w_gate.shape, BF16),
                pltpu.VMEM(w_out.shape, BF16),
                dma((6,)),
                pltpu.VMEM((SIDES, line, part_rows, cols4, chan), BF16),
                pltpu.VMEM((rows, cols, chan), BF16),
                pltpu.VMEM((quads, cols, lanes), BF16),
                pltpu.VMEM((SIDES, line, cols4, lanes), BF16),
                pltpu.VMEM((part_rows, chan, lanes), BF16),
                pltpu.VMEM((part_rows, chan, cols4), F32),
                pltpu.VMEM((part_rows, chan, cols4), F32),
                pltpu.VMEM((part_rows, 1, lanes), F32),
                pltpu.VMEM((part_rows, 1, lanes), F32),
                pltpu.VMEM((part_rows, cols4, chan), BF16),
                pltpu.VMEM((chan, chan), BF16),
                dma((PEERS,)),
                dma((PEERS,)),
                dma((2, 2, line)),
                dma((2, line)),
                dma((2, SIDES, line)),
                dma((SIDES, line)),
                dma((SIDES, line)),
                dma((SIDES, line, PEERS)),
                dma((SIDES, line, PEERS)),
                dma((PEERS,)),
                dma((PEERS,)),
            ],
            compiler_params=pltpu.CompilerParams(collective_id=0, has_side_effects=True),
            cost_estimate=pl.CostEstimate(flops=3 * 10**9, bytes_accessed=10**6, transcendentals=2 * 10**6),
        )(pair, w_query, w_kv, w_gate, w_out, pair_bias, lengths)

    in_specs = (P("grp", "col", None), P(), P(), P(), P(), P("grp", "col", None), P("grp"))
    return jax.shard_map(
        on_device, mesh=mesh, in_specs=in_specs, out_specs=P("grp", "col", None), check_vma=False
    )
```

```python
import functools

import jax
import jax.numpy as jnp
from jax import lax
from jax.experimental import pallas as pl
from jax.experimental.pallas import tpu as pltpu
from jax.sharding import PartitionSpec as P

HEADS = 4
MESH = pl.DeviceIdType.MESH
F32 = jnp.float32
BF16 = jnp.bfloat16
LOG2E = 1.4426950408889634
NT = (((1,), (1,)), ((), ()))
TN = (((0,), (0,)), ((), ()))


def dot(lhs, rhs):
    return jnp.dot(lhs, rhs, preferred_element_type=F32)


def dot_nt(lhs, rhs):
    return lax.dot_general(lhs, rhs, NT, preferred_element_type=F32)


def transposed(weight):
    return weight.astype(F32).T.astype(BF16)


def body(
    line, pair_in, wq_in, wkv_in, wg_in, wo_in, bias_in, len_ref, out_ref,
    pair_ref, bias_ref, wq_ref, wkv_ref, wg_ref, wo_ref, load_sem,
    gath, swap, bsend, bgath, bias_f, queries, gate, acc, run_max, run_sum, upd,
    wvt_ref, recv, zsend, nsend, fsend, bs_sem, br_sem, core_s, core_r,
):
    rows, cols, chan = pair_ref.shape
    half_rows, cols2 = rows // 2, 2 * cols
    quarter = half_rows // 2
    width = chan // HEADS
    lanes = HEADS * cols2
    chips = 4 * line

    me = lax.axis_index("col")
    core = lax.rem(me, 2)
    chip = me // 2
    z = chip // 4
    xy = lax.rem(chip, 4)
    sibling = me + 1 - 2 * core
    x_line = xy + 1 - 2 * lax.rem(xy, 2)
    y_line = lax.rem(xy + 2, 4)
    diag = 3 - xy
    near = (x_line, y_line)
    far = (y_line, x_line)

    def device(z_at, xy_at):
        return {"col": (z_at * 4 + xy_at) * 2 + core}

    loads = [
        pltpu.make_async_copy(source, target, load_sem.at[at])
        for at, (source, target) in enumerate((
            (pair_in, pair_ref), (bias_in, bias_ref), (wq_in, wq_ref),
            (wkv_in, wkv_ref), (wg_in, wg_ref), (wo_in, wo_ref),
        ))
    ]
    for load in loads:
        load.start()

    barrier = pltpu.get_barrier_semaphore()

    def greet(k, carry):
        other = lax.rem(chip + k, chips)
        pl.semaphore_signal(barrier, inc=1, device_id={"col": other * 2 + core}, device_id_type=MESH)
        return carry

    lax.fori_loop(1, chips, greet, 0)
    pl.semaphore_signal(barrier, inc=1, device_id={"col": sibling}, device_id_type=MESH)

    def normalized(first):
        values = pair_ref[pl.ds(first, half_rows)].astype(F32)
        centred = values - jnp.mean(values, axis=-1, keepdims=True)
        variance = jnp.mean(centred * centred, axis=-1, keepdims=True)
        return (centred * lax.rsqrt(variance + 1e-05)).astype(BF16)

    loads[0].wait()
    own_cols = pl.ds(pl.multiple_of(core * cols, cols), cols)
    swap[...] = normalized((1 - core) * half_rows)
    gath[xy, z, :, own_cols, :] = normalized(core * half_rows)

    pl.semaphore_wait(barrier, chips)

    swap_copy = pltpu.make_async_remote_copy(
        src_ref=swap, dst_ref=gath.at[xy, z, :, own_cols, :],
        send_sem=core_s.at[0], recv_sem=core_r.at[0],
        device_id={"col": sibling}, device_id_type=MESH,
    )
    swap_copy.start()

    loads[1].wait()
    low = lax.broadcasted_iota(jnp.int32, (cols, 2 * cols2), 1) < cols2
    for pair_at in range(chips // 2):
        parts = [
            bias_ref[h, :, pair_at * 2 * cols2 : (pair_at + 1) * 2 * cols2].astype(F32)
            for h in range(HEADS)
        ]
        rolled = [pltpu.roll(part, cols2, 1) for part in parts]
        for h in range(0, HEADS, 2):
            span = slice(h * cols2, (h + 2) * cols2)
            bsend[2 * pair_at, :, span] = jnp.where(low, parts[h], rolled[h + 1]).astype(BF16)
            bsend[2 * pair_at + 1, :, span] = jnp.where(low, rolled[h], parts[h + 1]).astype(BF16)

    swap_copy.wait_recv()

    def block_copy(half, xy_at, z_at, target, send_sem):
        block = gath.at[xy_at, z_at, pl.ds(half * quarter, quarter)]
        return pltpu.make_async_remote_copy(
            src_ref=block, dst_ref=block, send_sem=send_sem, recv_sem=recv.at[half, xy_at, z_at],
            device_id=target, device_id_type=MESH,
        )

    def up(half, z_at):
        return block_copy(half, xy, z_at, device(z + 1, xy), zsend.at[half, 0, z_at])

    def down(half, z_at):
        return block_copy(half, xy, z_at, device(z - 1, xy), zsend.at[half, 1, z_at])

    def to_near(half, z_at):
        return block_copy(half, xy, z_at, device(z, near[half]), nsend.at[half, z_at])

    def to_far(half, which, z_at):
        from_line = (xy, near[half])[which]
        return block_copy(half, from_line, z_at, device(z, far[half]), fsend.at[half, which, z_at])

    def arrived(half, xy_at, z_at):
        block_copy(half, xy_at, z_at, device(z, near[half]), nsend.at[half, z_at]).wait_recv()

    for half in range(2):
        pl.when(z + 1 < line)(lambda half=half: up(half, z).start())
        pl.when(z > 0)(lambda half=half: down(half, z).start())
        to_near(half, z).start()
        to_far(half, 0, z).start()

    def bias_copy(other, slot):
        return pltpu.make_async_remote_copy(
            src_ref=bsend.at[other], dst_ref=bgath.at[lax.rem(slot, 4), slot // 4, own_cols, :],
            send_sem=bs_sem.at[other], recv_sem=br_sem.at[slot],
            device_id={"col": other * 2 + core}, device_id_type=MESH,
        )

    def bias_peers(line_at, first, act):
        def one(k, carry):
            act(lax.rem(z + k, line) * 4 + line_at)
            return carry

        lax.fori_loop(first, line, one, 0)

    all_lines = ((xy, 1), (x_line, 0), (y_line, 0), (diag, 0))
    for line_at, first in all_lines:
        bias_peers(line_at, first, lambda other: bias_copy(other, chip).start())
    bgath[xy, z, own_cols, :] = bsend[chip]

    for load in loads[2:]:
        load.wait()
    wqt = transposed(wq_ref[...])
    wgt = transposed(wg_ref[...])
    wvt_ref[...] = transposed(wkv_ref[:, chan:])
    same_head = (
        lax.broadcasted_iota(jnp.int32, (chan, lanes), 0) // width
        == lax.broadcasted_iota(jnp.int32, (chan, lanes), 1) // cols2
    )

    def prepare(r, carry):
        own = gath[xy, z, r]
        repeated = jnp.concatenate([own] * HEADS, axis=0)
        own_query = (dot_nt(wqt, repeated) * width ** (-0.5)).astype(BF16).astype(F32)
        own_query = jnp.where(same_head, own_query, 0.0).astype(BF16)
        queries[r] = own_query
        gate[r] = jax.nn.sigmoid(dot_nt(wgt, own))
        return carry

    lax.fori_loop(0, half_rows, prepare, 0)

    def pass_far(half, z_at):
        arrived(half, near[half], z_at)
        to_far(half, 1, z_at).start()

    def pass_line(s):
        def lower():
            for half in range(2):
                arrived(half, xy, z - s)
                pl.when(z + 1 < line)(lambda: up(half, z - s).start())
                to_near(half, z - s).start()
                to_far(half, 0, z - s).start()

        def upper():
            for half in range(2):
                arrived(half, xy, z + s)
                pl.when(z > 0)(lambda: down(half, z + s).start())
                to_near(half, z + s).start()
                to_far(half, 0, z + s).start()

        pl.when(z >= s)(lower)
        pl.when(z + s < line)(upper)

    def pass_near(s):
        def lower():
            for half in range(2):
                pass_far(half, z - s)

        def upper():
            for half in range(2):
                pass_far(half, z + s)

        pl.when(z >= s)(lower)
        if s:
            pl.when(z + s < line)(upper)

    def bias_swap(at):
        line_at = all_lines[at][0]
        return pltpu.make_async_remote_copy(
            src_ref=bgath.at[line_at, :, own_cols, :], dst_ref=bgath.at[line_at, :, own_cols, :],
            send_sem=core_s.at[3 + at], recv_sem=core_r.at[3 + at],
            device_id={"col": sibling}, device_id_type=MESH,
        )

    def start_bias(at):
        line_at, first = all_lines[at]
        bias_peers(line_at, first, lambda other: bias_copy(other, other).wait_recv())
        bias_swap(at).start()

    limit = len_ref[0]

    def spread_bias(at):
        bias_swap(at).wait_recv()
        line_at = all_lines[at][0]

        def one(z_at, carry):
            first = (z_at * 4 + line_at) * cols2
            position = first + lax.broadcasted_iota(jnp.int32, (cols2, lanes), 0)
            mask = jnp.where(position < limit, 0.0, -1000000000.0)
            bias_f[line_at, z_at] = (bgath[line_at, z_at].astype(F32) + mask) * LOG2E
            return carry

        lax.fori_loop(0, line, one, 0)

    run_max[...] = jnp.full_like(run_max, -1e30)
    run_sum[...] = jnp.zeros_like(run_sum)
    acc[...] = jnp.zeros_like(acc)
    group = line // 2
    keys = group * cols2
    own_part = z // group
    per_pair = 2 * cols2

    def fold(half, line_at, part):
        first = half * quarter
        z_at = pl.ds(part * group, group)
        tiles = [gath[line_at, z_at, first + r].reshape(keys, chan) for r in range(quarter)]
        olds = [(run_max[first + r], run_sum[first + r], acc[first + r]) for r in range(quarter)]
        bias_tile = bias_f[line_at, z_at].reshape(keys, lanes)
        together = jnp.concatenate(tiles, axis=0)
        all_keys = dot(together, wkv_ref[:, :chan]).astype(BF16)
        all_values = dot_nt(wvt_ref[...], together).astype(BF16)
        news = []
        for r, (old_max, old_sum, old_acc) in enumerate(olds):
            span = slice(r * keys, (r + 1) * keys)
            scores = dot(all_keys[span], queries[first + r]) * LOG2E + bias_tile
            new_max = jnp.maximum(old_max, jnp.max(scores, axis=0, keepdims=True))
            rescale = jnp.exp2(old_max - new_max)
            expon = jnp.exp2(scores - new_max)
            total = old_sum * rescale + jnp.sum(expon, axis=0, keepdims=True)
            product = dot(all_values[:, span], expon.astype(BF16))
            result = []
            for h in range(HEADS):
                at = slice(h * width, (h + 1) * width)
                pair_of = slice((h // 2) * per_pair, (h // 2 + 1) * per_pair)
                result.append(old_acc[at] * rescale[:, pair_of] + product[at, pair_of])
            news.append((new_max, total, jnp.concatenate(result, axis=0)))
        for r, new in enumerate(news):
            run_max[first + r], run_sum[first + r], acc[first + r] = new

    def pick(half, lines):
        return jnp.where(half == 0, lines[0], lines[1])

    def fold_both(lines, part):
        def one(half, carry):
            fold(half, pick(half, lines), part)
            return carry

        lax.fori_loop(0, 2, one, 0)

    def late(unit, carry):
        half, stage = lax.rem(unit, 2), unit // 2
        line_at = jnp.where(stage < 2, pick(half, far), diag)
        part = jnp.where(lax.rem(stage, 2) == 0, own_part, 1 - own_part)
        for z_at in range(group):
            block = gath.at[line_at, part * group + z_at, pl.ds(half * quarter, quarter)]
            pltpu.make_async_copy(block, block, recv.at[half, line_at, part * group + z_at]).wait()
        fold(half, line_at, part)
        return carry

    own = (xy, xy)
    for s in range(1, line):
        pass_line(s)
        if s == group - 1 or line == 2:
            start_bias(0)
            pass_near(s - 1)
            spread_bias(0)
            fold_both(own, own_part)
        elif s == line - 2:
            start_bias(1)
            start_bias(2)
            pass_near(s - 1)
            spread_bias(1)
            spread_bias(2)
            fold_both(near, own_part)
            lax.fori_loop(0, 2, late, 0)
        else:
            pass_near(s - 1)
    start_bias(3)
    fold_both(own, 1 - own_part)
    pass_near(line - 1)
    spread_bias(3)
    fold_both(near, 1 - own_part)

    lax.fori_loop(2, 7, late, 0)

    other_cols = pl.ds(pl.multiple_of((1 - core) * cols, cols), cols)

    def out_copy(half):
        return pltpu.make_async_remote_copy(
            src_ref=upd.at[pl.ds(half * quarter, quarter), other_cols, :],
            dst_ref=out_ref.at[pl.ds(core * half_rows + half * quarter, quarter)],
            send_sem=core_s.at[1 + half], recv_sem=core_r.at[1 + half],
            device_id={"col": sibling}, device_id_type=MESH,
        )

    for half in range(2):
        if half:
            late(7, 0)
        hiddens = []
        for r in range(half * quarter, (half + 1) * quarter):
            scale = 1.0 / run_sum[r]
            parts = []
            for h in range(HEADS):
                block = acc[r, h * width : (h + 1) * width] * scale[:, (h // 2) * per_pair : (h // 2 + 1) * per_pair]
                if h % 2:
                    block = pltpu.roll(block, cols2, 1)
                parts.append(block[:, :cols2])
            attended = jnp.concatenate(parts, axis=0)
            hiddens.append((gate[r] * attended).T.astype(BF16))
        update = dot(jnp.concatenate(hiddens, axis=0), wo_ref[...]).astype(BF16)
        upd[pl.ds(half * quarter, quarter)] = update.reshape(quarter, cols2, chan)
        out_copy(half).start()
        out_ref[pl.ds(core * half_rows + half * quarter, quarter)] = upd[
            pl.ds(half * quarter, quarter), own_cols, :
        ]

    for half in range(2):
        out_copy(half).wait()
        for z_at in range(line):
            pl.when((z + 1 < line) & (z >= z_at))(lambda: up(half, z_at).wait_send())
            pl.when((z > 0) & (z <= z_at))(lambda: down(half, z_at).wait_send())
            to_near(half, z_at).wait_send()
            to_far(half, 0, z_at).wait_send()
            to_far(half, 1, z_at).wait_send()
    swap_copy.wait_send()
    for at, (line_at, first) in enumerate(all_lines):
        bias_peers(line_at, first, lambda other: bias_copy(other, chip).wait_send())
        bias_swap(at).wait_send()


def solution(mesh):
    chips = mesh.shape["col"] // 2
    line = chips // 4

    def on_device(pair, w_query, w_kv, w_gate, w_out, pair_bias, lengths):
        rows, cols, chan = pair.shape
        half_rows, cols2 = rows // 2, 2 * cols
        quarter = half_rows // 2
        lanes = HEADS * cols2
        vmem = pl.BlockSpec(memory_space=pltpu.VMEM)
        dma = pltpu.SemaphoreType.DMA
        return pl.pallas_call(
            functools.partial(body, line),
            out_shape=jax.ShapeDtypeStruct(pair.shape, BF16),
            in_specs=[pl.BlockSpec(memory_space=pl.ANY)] * 6 + [pl.BlockSpec(memory_space=pltpu.SMEM)],
            out_specs=vmem,
            scratch_shapes=[
                pltpu.VMEM(pair.shape, BF16),
                pltpu.VMEM(pair_bias.shape, BF16),
                pltpu.VMEM(w_query.shape, BF16),
                pltpu.VMEM(w_kv.shape, BF16),
                pltpu.VMEM(w_gate.shape, BF16),
                pltpu.VMEM(w_out.shape, BF16),
                dma((6,)),
                pltpu.VMEM((4, line, half_rows, cols2, chan), BF16),
                pltpu.VMEM((half_rows, cols, chan), BF16),
                pltpu.VMEM((chips, cols, lanes), BF16),
                pltpu.VMEM((4, line, cols2, lanes), BF16),
                pltpu.VMEM((4, line, cols2, lanes), F32),
                pltpu.VMEM((half_rows, chan, lanes), BF16),
                pltpu.VMEM((half_rows, chan, cols2), F32),
                pltpu.VMEM((half_rows, chan, 2 * cols2), F32),
                pltpu.VMEM((half_rows, 1, lanes), F32),
                pltpu.VMEM((half_rows, 1, lanes), F32),
                pltpu.VMEM((half_rows, cols2, chan), BF16),
                pltpu.VMEM((chan, chan), BF16),
                dma((2, 4, line)),
                dma((2, 2, line)),
                dma((2, line)),
                dma((2, 2, line)),
                dma((chips,)),
                dma((chips,)),
                dma((7,)),
                dma((7,)),
            ],
            compiler_params=pltpu.CompilerParams(
                collective_id=0, has_side_effects=True
            ),
            cost_estimate=pl.CostEstimate(flops=3 * 10**9, bytes_accessed=10**6, transcendentals=2 * 10**6),
        )(pair, w_query, w_kv, w_gate, w_out, pair_bias, lengths)

    in_specs = (P("grp", "col", None), P(), P(), P(), P(), P("grp", "col", None), P("grp"))
    return jax.shard_map(
        on_device, mesh=mesh, in_specs=in_specs, out_specs=P("grp", "col", None), check_vma=False
    )
```
